32 devices in a mesh: row: 8 (over z, core), col: 4 (over y, x).
Axes of the slice: x: 2, y: 2, z: 4, core: 2. Of those that a mesh axis runs over, the one named last changes fastest.
Arguments:
- buoy: bfloat16 [512, 512, 384], P('row', 'col'), may hold values from -6 to 6
- vel_w: bfloat16 [512, 512, 384], P('row', 'col'), may hold values from -6 to 6
- strat: float32 [576], P('col'), may hold values from 0.3 to 3
- eig_val: float32 [384], replicated, may hold values from 0.1 to 8
- eig_left: bfloat16 [384, 384], replicated, may hold values from -0.3125 to 0.3125
- eig_right: bfloat16 [384, 384], replicated, may hold values from -0.3125 to 0.3125
Outputs:
- new_buoy: bfloat16 [512, 512, 384], P('row', 'col')
- new_vel: bfloat16 [512, 512, 384], P('row', 'col')
The draws below stay inside these ranges and needn't reach their ends.
All inputs are finite; a program needn't handle non-finite values.
Results may differ from the reference program's by a relative error of at most 0.019.
The reference program's roundings to bfloat16 on the way count: a program that leaves them out, or rounds other values in their place, can miss the bound.
Values may be sent and summed in bfloat16 or wider, within the bound.
No kernel may reach another device: no remote copies, remote signals or barrier semaphores. Data moves between devices by JAX's collectives and lax.ppermute only.
A program may use at most 192 MiB of HBM per device.

```python
import math
import jax
import jax.numpy as jnp
from jax import lax

KX = 512
KY = 512
NZ = 384
XG = 768
YG = 768
ZG = 576


def shard_levels(own_key, extent, split, smallest, high):
    factor_of, own = 1.0, jax.random.fold_in(own_key, 6)
    for position, parts in split:
        steps = jnp.exp(jax.random.uniform(jax.random.fold_in(own, position), (parts,), jnp.float32, smallest / len(split), high / len(split)))
        factor_of = factor_of * jnp.repeat(steps, extent[position] // parts).reshape([-1 if axis == position else 1 for axis in range(len(extent))])
    return factor_of


def bell_draw(rng, dims, scale, reach, split=(), kind=jnp.bfloat16):
    values = scale * jax.random.normal(rng, dims, jnp.float32)
    if split:
        values = values * shard_levels(rng, dims, split, -0.22, 0.18)
    return jnp.clip(values, -reach, reach).astype(kind)


def setup_inputs(seed: int = 0) -> dict:
    key_list = jax.random.split(jax.random.key(seed), 7)
    buoy = bell_draw(key_list[0], (KX, KY, NZ), 1.0, 6.0, ((0, 8), (1, 4)))
    vel_w = bell_draw(key_list[1], (KX, KY, NZ), 1.0, 6.0, ((0, 8), (1, 4)))
    strat = jnp.clip(jnp.exp(math.log(3.0) - 2.3025851 * jax.random.uniform(key_list[2], (ZG,), jnp.float32) ** shard_levels(key_list[2], (ZG,), ((0, 4),), -0.2, 0.2)), 0.3, 3.0)
    eig_val = jnp.clip(jnp.exp(jax.random.uniform(key_list[3], (NZ,), jnp.float32, math.log(0.1), math.log(8.0))), 0.1, 8.0)
    eig_left = bell_draw(key_list[4], (NZ, NZ), NZ ** -0.5, 0.3125)
    eig_right = bell_draw(key_list[5], (NZ, NZ), NZ ** -0.5, 0.3125)
    return dict(buoy=buoy, vel_w=vel_w, strat=strat, eig_val=eig_val, eig_left=eig_left, eig_right=eig_right)


explicit_step = 0.5
diffuse_buoy = 0.5
diffuse_vel = 0.25
couple_buoy = 0.7
couple_vel = 0.7

def rounded(values):
    return lax.optimization_barrier(values.astype(jnp.bfloat16)).astype(jnp.float32)

def fourier_trig(modes, points):
    order = jnp.arange(modes, dtype=jnp.int32)
    freq = ((order + 1) // 2).astype(jnp.float32)
    place = jnp.arange(points, dtype=jnp.float32)
    angle = 2.0 * math.pi / points * freq[:, None] * place[None, :]
    return (order, jnp.where((order % 2 == 0)[:, None], jnp.cos(angle), jnp.sin(angle)))

def fourier_eval(modes, points):
    order, values = fourier_trig(modes, points)
    return (values * math.sqrt(2.0 / modes)).astype(jnp.bfloat16)

def fourier_proj(modes, points):
    order, values = fourier_trig(modes, points)
    weight = jnp.where(order == 0, 1.0 / points, 2.0 / points).astype(jnp.float32)
    return jnp.transpose(values * weight[:, None] * math.sqrt(modes / 2.0)).astype(jnp.bfloat16)

def cheb_tables(degree, points):
    order = jnp.arange(degree, dtype=jnp.float32)
    theta = math.pi * (jnp.arange(points, dtype=jnp.float32) + 0.5) / points
    angle = order[:, None] * theta[None, :]
    norm = math.sqrt(2.0 / degree)
    levels = jnp.cos(angle) * norm
    slopes = -(order[:, None] / degree) * jnp.sin(angle) * norm
    weight = jnp.where(order == 0, 1.0 / points, 2.0 / points).astype(jnp.float32)
    projector = jnp.transpose(jnp.cos(angle) * weight[:, None] * math.sqrt(degree / 2.0))
    return (levels.astype(jnp.bfloat16), slopes.astype(jnp.bfloat16), projector.astype(jnp.bfloat16))

def wave_squares(modes):
    order = jnp.arange(modes, dtype=jnp.int32)
    freq = ((order + 1) // 2).astype(jnp.float32) * (2.0 / modes)
    return freq * freq

def mult(form, left, right):
    return jnp.einsum(form, left, right, precision=lax.Precision.HIGHEST)

def reference(buoy, vel_w, strat, eig_val, eig_left, eig_right):
    levels, slopes, projector = cheb_tables(NZ, ZG)
    along_y = fourier_eval(KY, YG).astype(jnp.float32)
    along_x = fourier_eval(KX, XG).astype(jnp.float32)
    back_x = fourier_proj(KX, XG).astype(jnp.float32)
    back_y = fourier_proj(KY, YG).astype(jnp.float32)
    vel_full = vel_w.astype(jnp.float32)
    buoy_full = buoy.astype(jnp.float32)
    depth = ZG // 8

    def slab(carry, block):
        start = (block * depth).astype(jnp.int32)
        level_part = lax.dynamic_slice_in_dim(levels, start, depth, 1).astype(jnp.float32)
        slope_part = lax.dynamic_slice_in_dim(slopes, start, depth, 1).astype(jnp.float32)
        proj_part = lax.dynamic_slice_in_dim(projector, start, depth, 0).astype(jnp.float32)
        strata = lax.dynamic_slice_in_dim(strat, start, depth, 0)
        field_list = []
        for coeffs, lookup in ((vel_full, level_part), (buoy_full, slope_part)):
            upper = rounded(mult('xyn,nz->xyz', coeffs, lookup))
            middle = rounded(mult('xkz,ky->xyz', upper, along_y))
            field_list.append(rounded(mult('kyz,kx->xyz', middle, along_x)))
        vel_grid, slope_grid = field_list
        flux_buoy = rounded(-(vel_grid * slope_grid) - strata[None, None, :] * vel_grid)
        flux_vel = rounded(-(vel_grid * jnp.abs(vel_grid)))
        totals = []
        for flux, total in ((flux_buoy, carry[0]), (flux_vel, carry[1])):
            partial_x = rounded(mult('xyz,xk->kyz', flux, back_x))
            partial_y = rounded(mult('kyz,yl->klz', partial_x, back_y))
            totals.append(total + mult('klz,zn->kln', partial_y, proj_part))
        return ((totals[0], totals[1]), None)
    zeros = jnp.zeros((KX, KY, NZ), jnp.float32)
    (tend_buoy, tend_vel), _ = lax.scan(slab, (zeros, zeros), jnp.arange(ZG // depth, dtype=jnp.int32))
    rhs_buoy = rounded(buoy_full + explicit_step * tend_buoy)
    rhs_vel = rounded(vel_full + explicit_step * tend_vel)
    left_matrix = eig_left.astype(jnp.float32)
    modal_buoy = mult('xyn,nj->xyj', rhs_buoy, left_matrix)
    modal_vel = mult('xyn,nj->xyj', rhs_vel, left_matrix)
    lapl = 4.0 * (wave_squares(KX)[:, None, None] + wave_squares(KY)[None, :, None]) + eig_val[None, None, :]
    diag_buoy = 1.0 + diffuse_buoy * lapl
    diag_vel = 1.0 + diffuse_vel * lapl
    determ = diag_buoy * diag_vel + couple_buoy * couple_vel
    solved_buoy = rounded((diag_vel * modal_buoy - couple_buoy * modal_vel) / determ)
    solved_vel = rounded((diag_buoy * modal_vel + couple_vel * modal_buoy) / determ)
    right_matrix = eig_right.astype(jnp.float32)
    new_buoy = mult('xyj,jn->xyn', solved_buoy, right_matrix).astype(jnp.bfloat16)
    new_vel = mult('xyj,jn->xyn', solved_vel, right_matrix).astype(jnp.bfloat16)
    return (new_buoy, new_vel)
```

```python
import math

import jax
import jax.numpy as jnp
import numpy as np
from jax import lax
from jax.experimental import pallas as pl
from jax.experimental.pallas import tpu as pltpu
from jax.sharding import PartitionSpec as P

explicit_step = 0.5
diffuse_buoy = 0.5
diffuse_vel = 0.25
couple_buoy = 0.7
couple_vel = 0.7

CHUNKS = 4
BF16 = jnp.bfloat16
F32 = jnp.float32
VMEM_BYTES = 56 * 1024 * 1024


def fourier_trig(modes, points):
    order = np.arange(modes, dtype=np.int32)
    freq = ((order + 1) // 2).astype(np.float32)
    place = np.arange(points, dtype=np.float32)
    angle = np.float32(2.0 * math.pi / points) * freq[:, None] * place[None, :]
    return (order, np.where((order % 2 == 0)[:, None], np.cos(angle), np.sin(angle)))


def fourier_eval(modes, points):
    order, values = fourier_trig(modes, points)
    return (values * np.float32(math.sqrt(2.0 / modes))).astype(BF16)


def fourier_proj(modes, points):
    order, values = fourier_trig(modes, points)
    weight = np.where(order == 0, 1.0 / points, 2.0 / points).astype(np.float32)
    return np.transpose(values * weight[:, None] * np.float32(math.sqrt(modes / 2.0))).astype(BF16)


def cheb_tables(degree, points):
    order = np.arange(degree, dtype=np.float32)
    theta = np.float32(math.pi) * (np.arange(points, dtype=np.float32) + np.float32(0.5)) / np.float32(points)
    angle = order[:, None] * theta[None, :]
    norm = np.float32(math.sqrt(2.0 / degree))
    levels = np.cos(angle) * norm
    slopes = -(order[:, None] / np.float32(degree)) * np.sin(angle) * norm
    weight = np.where(order == 0, 1.0 / points, 2.0 / points).astype(np.float32)
    projector = np.transpose(np.cos(angle) * weight[:, None] * np.float32(math.sqrt(degree / 2.0)))
    return (levels.astype(BF16), slopes.astype(BF16), projector.astype(BF16))


def wave_squares(modes, offset, count):
    order = offset + jnp.arange(count, dtype=jnp.int32)
    freq = ((order + 1) // 2).astype(F32) * (2.0 / modes)
    return freq * freq


def largest_divisor(count, limit):
    return max(size for size in range(1, limit + 1) if count % size == 0)


def params(grid_rank):
    return pltpu.CompilerParams(
        dimension_semantics=("arbitrary",) * grid_rank, vmem_limit_bytes=VMEM_BYTES
    )


def whole(shape):
    return pl.BlockSpec(shape, lambda *_: (0,) * len(shape))


def lift_kernel(vel_ref, buoy_ref, table_ref, out_ref):
    blocks, fields, depth, span, lanes = out_ref.shape
    for field, source in enumerate((vel_ref, buoy_ref)):
        coeffs = source[...].reshape(span * lanes, source.shape[-1])
        values = lax.dot_general(
            table_ref[field], coeffs, (((1,), (1,)), ((), ())), preferred_element_type=F32
        )
        values = values.reshape(blocks * depth, span, lanes).astype(BF16)
        out_ref[:, field] = values.reshape(blocks, depth, span, lanes)


def lift(kernels, vel_w, buoy, table, blocks):
    modes_x, modes_y, degree = vel_w.shape
    depth = table.shape[1] // blocks
    shape = (blocks, 2, depth, modes_x, modes_y)
    if not kernels:
        fields = jnp.stack([vel_w, buoy])
        values = jnp.einsum("fzn,fakn->fzak", table, fields, preferred_element_type=F32)
        values = values.astype(BF16).reshape(2, blocks, depth, modes_x, modes_y)
        return jnp.transpose(values, (1, 0, 2, 3, 4))
    span = 16
    return pl.pallas_call(
        lift_kernel,
        grid=(modes_x // span,),
        in_specs=[
            pl.BlockSpec((span, modes_y, degree), lambda a: (a, 0, 0)),
            pl.BlockSpec((span, modes_y, degree), lambda a: (a, 0, 0)),
            whole(table.shape),
        ],
        out_specs=pl.BlockSpec((blocks, 2, depth, span, modes_y), lambda a: (0, 0, 0, a, 0)),
        out_shape=jax.ShapeDtypeStruct(shape, BF16),
        compiler_params=params(1),
        cost_estimate=pl.CostEstimate(
            flops=2 * math.prod(shape) * degree,
            bytes_accessed=2 * (2 * vel_w.size + math.prod(shape)),
            transcendentals=0,
        ),
        name="lift",
    )(vel_w, buoy, table)


def spread_kernel(in_ref, table_ref, *out_refs):
    blocks, _, depth, modes_x, lanes = in_ref.shape
    parts = [in_ref[:, 0, level].reshape(blocks * modes_x, lanes) for level in range(depth)]
    values = jnp.dot(
        table_ref[...], jnp.concatenate(parts, axis=1), preferred_element_type=F32
    ).astype(BF16)
    rows = out_refs[0].shape[2]
    for position, out_ref in enumerate(out_refs):
        for level in range(depth):
            out_ref[0, level] = values[
                position * rows : (position + 1) * rows, level * lanes : (level + 1) * lanes
            ]


def spread(kernels, arrived, table, col_count):
    blocks, fields, depth, modes_x, modes_y = arrived.shape
    rows = table.shape[0] // col_count
    if not kernels:
        values = jnp.einsum(
            "xpa,pfzak->fzxk",
            table.reshape(-1, blocks, modes_x),
            arrived,
            preferred_element_type=F32,
        ).astype(BF16)
        return [values[:, :, c * rows : (c + 1) * rows] for c in range(col_count)]
    step = largest_divisor(depth, 6)
    shape = (fields, depth, rows, modes_y)
    return pl.pallas_call(
        spread_kernel,
        grid=(fields, depth // step),
        in_specs=[
            pl.BlockSpec((blocks, 1, step, modes_x, modes_y), lambda f, z: (0, f, z, 0, 0)),
            whole(table.shape),
        ],
        out_specs=[pl.BlockSpec((1, step, rows, modes_y), lambda f, z: (f, z, 0, 0))] * col_count,
        out_shape=[jax.ShapeDtypeStruct(shape, BF16)] * col_count,
        compiler_params=params(2),
        cost_estimate=pl.CostEstimate(
            flops=2 * fields * depth * modes_y * table.size,
            bytes_accessed=2 * (arrived.size + col_count * math.prod(shape)),
            transcendentals=0,
        ),
        name="spread",
    )(arrived, table)


def flux_kernel(count, strat_ref, along_ref, back_ref, *refs):
    in_refs, out_refs = refs[:count], refs[count:]
    _, depth, rows, lanes = in_refs[0].shape
    grids = []
    for field in range(2):
        parts = [ref[field].reshape(depth * rows, lanes) for ref in in_refs]
        grids.append(
            jnp.dot(
                jnp.concatenate(parts, axis=1), along_ref[...], preferred_element_type=F32
            ).astype(BF16)
        )
    first = pl.program_id(0) * depth
    buoy_parts, vel_parts = [], []
    for level in range(depth):
        velocity = grids[0][level * rows : (level + 1) * rows].astype(F32)
        gradient = grids[1][level * rows : (level + 1) * rows].astype(F32)
        flux_buoy = -(velocity * gradient) - strat_ref[first + level] * velocity
        buoy_parts.append(flux_buoy.astype(BF16))
        vel_parts.append((-(velocity * jnp.abs(velocity))).astype(BF16))
    for field, parts in enumerate((buoy_parts, vel_parts)):
        values = jnp.dot(
            jnp.concatenate(parts, axis=0), back_ref[...], preferred_element_type=F32
        ).astype(BF16)
        for position, ref in enumerate(out_refs):
            ref[field] = values[:, position * lanes : (position + 1) * lanes].reshape(
                depth, rows, lanes
            )


def make_fluxes(kernels, arrived, strat, along_y, back_y):
    count = len(arrived)
    fields, depth, rows, lanes = arrived[0].shape
    if not kernels:
        values = jnp.concatenate(arrived, axis=-1)
        grids = jnp.einsum("fzxk,ky->fzxy", values, along_y, preferred_element_type=F32)
        grids = grids.astype(BF16).astype(F32)
        flux_buoy = -(grids[0] * grids[1]) - strat[:, None, None] * grids[0]
        flux_vel = -(grids[0] * jnp.abs(grids[0]))
        fluxes = jnp.stack([flux_buoy, flux_vel]).astype(BF16)
        values = jnp.einsum("fzxy,yk->fzxk", fluxes, back_y, preferred_element_type=F32)
        return jnp.split(values.astype(BF16), count, axis=-1)
    step = largest_divisor(depth, 3)
    block = pl.BlockSpec((fields, step, rows, lanes), lambda z: (0, z, 0, 0))
    return pl.pallas_call(
        lambda *refs: flux_kernel(count, *refs),
        grid=(depth // step,),
        in_specs=[pl.BlockSpec(memory_space=pltpu.SMEM), whole(along_y.shape), whole(back_y.shape)]
        + [block] * count,
        out_specs=[block] * count,
        out_shape=[jax.ShapeDtypeStruct(arrived[0].shape, BF16)] * count,
        compiler_params=params(1),
        cost_estimate=pl.CostEstimate(
            flops=4 * fields * depth * rows * along_y.size,
            bytes_accessed=4 * count * arrived[0].size,
            transcendentals=0,
        ),
        name="fluxes",
    )(strat, along_y, back_y, *arrived)


def fold_kernel(count, table_ref, *refs):
    in_refs, out_ref = refs[:count], refs[count]
    blocks, _, depth, modes_x, lanes = out_ref.shape
    parts = [
        jnp.concatenate([ref[0, level] for ref in in_refs], axis=0) for level in range(depth)
    ]
    values = jnp.dot(
        table_ref[...], jnp.concatenate(parts, axis=1), preferred_element_type=F32
    ).astype(BF16)
    for level in range(depth):
        out_ref[:, 0, level] = values[:, level * lanes : (level + 1) * lanes].reshape(
            blocks, modes_x, lanes
        )


def fold(kernels, arrived, table, blocks):
    count = len(arrived)
    fields, depth, rows, lanes = arrived[0].shape
    modes_x = table.shape[0] // blocks
    if not kernels:
        values = jnp.einsum(
            "pax,fzxk->pfzak",
            table.reshape(blocks, modes_x, -1),
            jnp.concatenate(arrived, axis=2),
            preferred_element_type=F32,
        )
        return values.astype(BF16)
    step = largest_divisor(depth, 6)
    shape = (blocks, fields, depth, modes_x, lanes)
    return pl.pallas_call(
        lambda *refs: fold_kernel(count, *refs),
        grid=(fields, depth // step),
        in_specs=[whole(table.shape)]
        + [pl.BlockSpec((1, step, rows, lanes), lambda f, z: (f, z, 0, 0))] * count,
        out_specs=pl.BlockSpec((blocks, 1, step, modes_x, lanes), lambda f, z: (0, f, z, 0, 0)),
        out_shape=jax.ShapeDtypeStruct(shape, BF16),
        compiler_params=params(2),
        cost_estimate=pl.CostEstimate(
            flops=2 * fields * depth * lanes * table.size,
            bytes_accessed=2 * (count * arrived[0].size + math.prod(shape)),
            transcendentals=0,
        ),
        name="fold",
    )(table, *arrived)


def solve_modal(modal_buoy, modal_vel, wave, eig_val):
    lapl = wave + eig_val
    diag_buoy = 1.0 + diffuse_buoy * lapl
    diag_vel = 1.0 + diffuse_vel * lapl
    scale = 1.0 / (diag_buoy * diag_vel + couple_buoy * couple_vel)
    solved_buoy = ((diag_vel * modal_buoy - couple_buoy * modal_vel) * scale).astype(BF16)
    solved_vel = ((diag_buoy * modal_vel + couple_vel * modal_buoy) * scale).astype(BF16)
    return (solved_buoy, solved_vel)


def finish_kernel(
    wave_x_ref, wave_y_ref, eig_val_ref, left_ref, right_ref, proj_ref, buoy_ref, vel_ref, *refs
):
    in_refs, out_refs = refs[:-2], refs[-2:]
    span, lanes, degree = buoy_ref.shape
    modal = []
    for field, coeff_ref in enumerate((buoy_ref, vel_ref)):
        parts = []
        for ref in in_refs:
            part = ref[:, field]
            parts.append(part.reshape(part.shape[0] * part.shape[1], span, lanes))
        fluxes = jnp.concatenate(parts, axis=0).astype(F32)
        fluxes = jnp.swapaxes(fluxes, 0, 1).astype(BF16)
        rows = []
        for mode in range(span):
            tend = lax.dot_general(
                fluxes[mode], proj_ref[...], (((0,), (0,)), ((), ())), preferred_element_type=F32
            )
            rows.append((coeff_ref[mode].astype(F32) + explicit_step * tend).astype(BF16))
        modal.append(
            jnp.dot(jnp.concatenate(rows, axis=0), left_ref[...], preferred_element_type=F32)
        )
    first = pl.program_id(0) * span
    waves = [4.0 * (wave_x_ref[first + mode] + wave_y_ref[...]) for mode in range(span)]
    solved = solve_modal(modal[0], modal[1], jnp.concatenate(waves, axis=0), eig_val_ref[...])
    for values, out_ref in zip(solved, out_refs):
        result = jnp.dot(values, right_ref[...], preferred_element_type=F32).astype(BF16)
        out_ref[...] = result.reshape(span, lanes, degree)


def finish(kernels, folded, buoy, vel_w, projs, eig_val, eig_left, eig_right, wave_x, wave_y):
    modes_x, modes_y, degree = buoy.shape
    if not kernels:
        tend = 0.0
        for part, proj in zip(folded, projs):
            parts = jnp.transpose(part, (1, 0, 2, 3, 4)).reshape(2, -1, modes_x, modes_y)
            tend += jnp.einsum("fzak,zn->fakn", parts, proj, preferred_element_type=F32)
        modal = []
        for field, coeffs in enumerate((buoy, vel_w)):
            rhs = (coeffs.astype(F32) + explicit_step * tend[field]).astype(BF16)
            modal.append(jnp.einsum("akn,nj->akj", rhs, eig_left, preferred_element_type=F32))
        wave = 4.0 * (wave_x[:, None, None] + wave_y[None, :, None])
        solved = solve_modal(modal[0], modal[1], wave, eig_val)
        return tuple(
            jnp.einsum("akj,jn->akn", values, eig_right, preferred_element_type=F32).astype(BF16)
            for values in solved
        )
    span = 8
    proj = jnp.concatenate(projs, axis=0)
    field_block = pl.BlockSpec((span, modes_y, degree), lambda a: (a, 0, 0))
    result = jax.ShapeDtypeStruct(buoy.shape, BF16)
    return pl.pallas_call(
        finish_kernel,
        grid=(modes_x // span,),
        in_specs=[
            pl.BlockSpec(memory_space=pltpu.SMEM),
            whole((modes_y, 1)),
            whole((1, degree)),
            whole(eig_left.shape),
            whole(eig_right.shape),
            whole(proj.shape),
            field_block,
            field_block,
        ]
        + [
            pl.BlockSpec(
                (part.shape[0], 2, part.shape[2], span, modes_y), lambda a: (0, 0, 0, a, 0)
            )
            for part in folded
        ],
        out_specs=[field_block, field_block],
        out_shape=[result, result],
        compiler_params=params(1),
        cost_estimate=pl.CostEstimate(
            flops=4 * buoy.size * (proj.shape[0] + 2 * degree),
            bytes_accessed=8 * buoy.size + sum(2 * part.size for part in folded),
            transcendentals=buoy.size,
        ),
        name="finish",
    )(
        wave_x,
        wave_y[:, None],
        eig_val[None, :],
        eig_left,
        eig_right,
        proj,
        buoy,
        vel_w,
        *folded,
    )


def per_device(buoy, vel_w, strat, eig_val, eig_left, eig_right):
    row_count = lax.axis_size("row")
    col_count = lax.axis_size("col")
    modes_x, modes_y, degree = buoy.shape
    total_x, total_y = modes_x * row_count, modes_y * col_count
    grid_x, grid_y = 3 * total_x // 2, 3 * total_y // 2
    grid_z = strat.shape[0] * col_count
    own = grid_z // row_count
    rows_x = grid_x // col_count
    kernels = modes_y % 128 == 0 and modes_x % 16 == 0 and rows_x % 16 == 0 and degree % 128 == 0
    paired = col_count & (col_count - 1) == 0

    def partner(device, shift, sign):
        return device ^ shift if paired else (device + sign * shift) % col_count

    row = lax.axis_index("row")
    col = lax.axis_index("col")
    shifts = np.arange(col_count)
    sends = [[partner(c, s, 1) for s in shifts] for c in range(col_count)]
    receives = [[partner(c, s, -1) for s in shifts] for c in range(col_count)]
    send_order = jnp.asarray(np.array(sends, np.int32))[col]
    receive_order = jnp.asarray(np.array(receives, np.int32))[col]

    def exchange_col(blocks):
        arrived = [blocks[0]]
        for shift in range(1, col_count):
            pairs = [(c, int(partner(c, shift, 1))) for c in range(col_count)]
            arrived.append(lax.ppermute(blocks[shift], "col", pairs))
        return arrived

    def exchange_row(values):
        return lax.all_to_all(values, "row", split_axis=0, concat_axis=0, tiled=True)

    levels, slopes, projector = cheb_tables(degree, grid_z)
    forward_z = np.stack([levels.T, slopes.T]).reshape(2, row_count, own, degree)
    backward_z = projector.reshape(row_count, own, degree)
    along_x = jnp.asarray(fourier_eval(total_x, grid_x).T.reshape(col_count, rows_x, total_x))
    along_x = along_x[send_order].reshape(grid_x, total_x)
    back_x = jnp.asarray(fourier_proj(total_x, grid_x).T.reshape(total_x, col_count, rows_x))
    back_x = back_x[:, receive_order].reshape(total_x, grid_x)
    along_y = jnp.asarray(fourier_eval(total_y, grid_y).reshape(col_count, modes_y, grid_y))
    along_y = along_y[receive_order].reshape(total_y, grid_y)
    back_y = jnp.asarray(fourier_proj(total_y, grid_y).reshape(grid_y, col_count, modes_y))
    back_y = back_y[:, send_order].reshape(grid_y, total_y)
    strat_all = lax.all_gather(strat, "col", axis=0, tiled=True)
    strat_own = lax.dynamic_slice_in_dim(strat_all, row * own, own)

    depth = own // CHUNKS if own % CHUNKS == 0 else own
    starts = list(range(0, own, depth))
    folded, projs = [], []
    for start in starts:
        table = jnp.asarray(
            forward_z[:, :, start : start + depth].reshape(2, row_count * depth, degree)
        )
        projs.append(
            jnp.asarray(backward_z[:, start : start + depth].reshape(row_count * depth, degree))
        )
        lifted = exchange_row(lift(kernels, vel_w, buoy, table, row_count))
        arrived = exchange_col(spread(kernels, lifted, along_x, col_count))
        fluxes = make_fluxes(
            kernels, arrived, strat_own[start : start + depth], along_y, back_y
        )
        returned = exchange_col(fluxes)
        folded.append(exchange_row(fold(kernels, returned, back_x, row_count)))
    wave_x = wave_squares(total_x, row * modes_x, modes_x)
    wave_y = wave_squares(total_y, col * modes_y, modes_y)
    return finish(
        kernels, folded, buoy, vel_w, projs, eig_val, eig_left, eig_right, wave_x, wave_y
    )


def solution(mesh):
    in_specs = (P("row", "col", None), P("row", "col", None), P("col"), P(), P(), P())
    out_specs = (P("row", "col", None), P("row", "col", None))
    return jax.shard_map(
        per_device, mesh=mesh, in_specs=in_specs, out_specs=out_specs, check_vma=False
    )
```

```python
import math

import jax
import jax.numpy as jnp
import numpy as np
from jax import lax
from jax.experimental import pallas as pl
from jax.experimental.pallas import tpu as pltpu
from jax.sharding import PartitionSpec as P

explicit_step = 0.5
diffuse_buoy = 0.5
diffuse_vel = 0.25
couple_buoy = 0.7
couple_vel = 0.7

BF16 = jnp.bfloat16
F32 = jnp.float32
VMEM_BYTES = 56 * 1024 * 1024


def fourier_trig(modes, points):
    order = np.arange(modes, dtype=np.int32)
    freq = ((order + 1) // 2).astype(np.float32)
    place = np.arange(points, dtype=np.float32)
    angle = np.float32(2.0 * math.pi / points) * freq[:, None] * place[None, :]
    return (order, np.where((order % 2 == 0)[:, None], np.cos(angle), np.sin(angle)))


def fourier_eval(modes, points):
    order, values = fourier_trig(modes, points)
    return (values * np.float32(math.sqrt(2.0 / modes))).astype(BF16)


def fourier_proj(modes, points):
    order, values = fourier_trig(modes, points)
    weight = np.where(order == 0, 1.0 / points, 2.0 / points).astype(np.float32)
    return np.transpose(values * weight[:, None] * np.float32(math.sqrt(modes / 2.0))).astype(BF16)


def cheb_tables(degree, points):
    order = np.arange(degree, dtype=np.float32)
    theta = np.float32(math.pi) * (np.arange(points, dtype=np.float32) + np.float32(0.5)) / np.float32(points)
    angle = order[:, None] * theta[None, :]
    norm = np.float32(math.sqrt(2.0 / degree))
    levels = np.cos(angle) * norm
    slopes = -(order[:, None] / np.float32(degree)) * np.sin(angle) * norm
    weight = np.where(order == 0, 1.0 / points, 2.0 / points).astype(np.float32)
    projector = np.transpose(np.cos(angle) * weight[:, None] * np.float32(math.sqrt(degree / 2.0)))
    return (levels.astype(BF16), slopes.astype(BF16), projector.astype(BF16))


def wave_squares(modes, offset, count):
    order = offset + jnp.arange(count, dtype=jnp.int32)
    freq = ((order + 1) // 2).astype(F32) * (2.0 / modes)
    return freq * freq


def params(grid_rank):
    return pltpu.CompilerParams(
        dimension_semantics=("arbitrary",) * grid_rank, vmem_limit_bytes=VMEM_BYTES
    )


def whole(shape):
    return pl.BlockSpec(shape, lambda *_: (0,) * len(shape))


def lift_kernel(vel_ref, buoy_ref, table_ref, out_ref):
    blocks, fields, depth, span, lanes = out_ref.shape
    for field, source in enumerate((vel_ref, buoy_ref)):
        coeffs = source[...].reshape(span * lanes, source.shape[-1])
        values = lax.dot_general(
            table_ref[field], coeffs, (((1,), (1,)), ((), ())), preferred_element_type=F32
        )
        values = values.reshape(blocks * depth, span, lanes).astype(BF16)
        out_ref[:, field] = values.reshape(blocks, depth, span, lanes)


def lift(kernels, vel_w, buoy, table, blocks):
    modes_x, modes_y, degree = vel_w.shape
    depth = table.shape[1] // blocks
    shape = (blocks, 2, depth, modes_x, modes_y)
    if not kernels:
        fields = jnp.stack([vel_w, buoy])
        values = jnp.einsum("fzn,fakn->fzak", table, fields, preferred_element_type=F32)
        values = values.astype(BF16).reshape(2, blocks, depth, modes_x, modes_y)
        return jnp.transpose(values, (1, 0, 2, 3, 4))
    span = 16
    return pl.pallas_call(
        lift_kernel,
        grid=(modes_x // span,),
        in_specs=[
            pl.BlockSpec((span, modes_y, degree), lambda a: (a, 0, 0)),
            pl.BlockSpec((span, modes_y, degree), lambda a: (a, 0, 0)),
            whole(table.shape),
        ],
        out_specs=pl.BlockSpec((blocks, 2, depth, span, modes_y), lambda a: (0, 0, 0, a, 0)),
        out_shape=jax.ShapeDtypeStruct(shape, BF16),
        compiler_params=params(1),
        cost_estimate=pl.CostEstimate(
            flops=2 * math.prod(shape) * degree,
            bytes_accessed=2 * (2 * vel_w.size + math.prod(shape)),
            transcendentals=0,
        ),
        name="lift",
    )(vel_w, buoy, table)


def plane_kernel(
    col_count, strat_ref, along_y_ref, along_x_ref, back_x_ref, back_y_ref, in_ref, out_ref
):
    blocks, _, depth, modes_x, lanes = in_ref.shape
    row_count = blocks // col_count
    for level in range(depth):
        grids = []
        for field in range(2):
            rows = []
            for row in range(row_count):
                parts = [in_ref[row * col_count + col, field, level] for col in range(col_count)]
                rows.append(jnp.concatenate(parts, axis=1))
            middle = jnp.dot(
                jnp.concatenate(rows, axis=0), along_y_ref[...], preferred_element_type=F32
            ).astype(BF16)
            grid = jnp.dot(along_x_ref[...], middle, preferred_element_type=F32)
            grids.append(grid.astype(BF16).astype(F32))
        velocity, gradient = grids
        strata = strat_ref[pl.program_id(0) * depth + level]
        flux_buoy = (-(velocity * gradient) - strata * velocity).astype(BF16)
        flux_vel = (-(velocity * jnp.abs(velocity))).astype(BF16)
        for field, flux in enumerate((flux_buoy, flux_vel)):
            folded = jnp.dot(back_x_ref[...], flux, preferred_element_type=F32).astype(BF16)
            values = jnp.dot(folded, back_y_ref[...], preferred_element_type=F32).astype(BF16)
            for row in range(row_count):
                for col in range(col_count):
                    out_ref[row * col_count + col, field, level] = values[
                        row * modes_x : (row + 1) * modes_x, col * lanes : (col + 1) * lanes
                    ]


def planes(kernels, arrived, strat, along_y, along_x, back_x, back_y, col_count):
    blocks, fields, depth, modes_x, modes_y = arrived.shape
    row_count = blocks // col_count
    if not kernels:
        parts = arrived.reshape(row_count, col_count, fields, depth, modes_x, modes_y)
        parts = jnp.transpose(parts, (2, 3, 0, 4, 1, 5))
        parts = parts.reshape(fields, depth, row_count * modes_x, col_count * modes_y)
        middle = jnp.einsum("fzak,ky->fzay", parts, along_y, preferred_element_type=F32)
        grids = jnp.einsum("xa,fzay->fzxy", along_x, middle.astype(BF16), preferred_element_type=F32)
        grids = grids.astype(BF16).astype(F32)
        flux_buoy = -(grids[0] * grids[1]) - strat[:, None, None] * grids[0]
        flux_vel = -(grids[0] * jnp.abs(grids[0]))
        fluxes = jnp.stack([flux_buoy, flux_vel]).astype(BF16)
        folded = jnp.einsum("ax,fzxy->fzay", back_x, fluxes, preferred_element_type=F32)
        values = jnp.einsum("fzay,yk->fzak", folded.astype(BF16), back_y, preferred_element_type=F32)
        values = values.astype(BF16).reshape(
            fields, depth, row_count, modes_x, col_count, modes_y
        )
        return jnp.transpose(values, (2, 4, 0, 1, 3, 5)).reshape(arrived.shape)
    block = pl.BlockSpec((blocks, fields, 1, modes_x, modes_y), lambda z: (0, 0, z, 0, 0))
    work = along_y.size * along_x.shape[1] + along_x.size * along_y.shape[1]
    return pl.pallas_call(
        lambda *refs: plane_kernel(col_count, *refs),
        grid=(depth,),
        in_specs=[
            pl.BlockSpec(memory_space=pltpu.SMEM),
            whole(along_y.shape),
            whole(along_x.shape),
            whole(back_x.shape),
            whole(back_y.shape),
            block,
        ],
        out_specs=block,
        out_shape=jax.ShapeDtypeStruct(arrived.shape, BF16),
        compiler_params=params(1),
        cost_estimate=pl.CostEstimate(
            flops=4 * fields * depth * work, bytes_accessed=4 * arrived.size, transcendentals=0
        ),
        name="planes",
    )(strat, along_y, along_x, back_x, back_y, arrived)


def solve_modal(modal_buoy, modal_vel, wave, eig_val):
    lapl = wave + eig_val
    diag_buoy = 1.0 + diffuse_buoy * lapl
    diag_vel = 1.0 + diffuse_vel * lapl
    scale = 1.0 / (diag_buoy * diag_vel + couple_buoy * couple_vel)
    solved_buoy = ((diag_vel * modal_buoy - couple_buoy * modal_vel) * scale).astype(BF16)
    solved_vel = ((diag_buoy * modal_vel + couple_vel * modal_buoy) * scale).astype(BF16)
    return (solved_buoy, solved_vel)


def finish_kernel(
    wave_x_ref, wave_y_ref, eig_val_ref, left_ref, right_ref, proj_ref, buoy_ref, vel_ref, *refs
):
    in_refs, out_refs = refs[:-2], refs[-2:]
    span, lanes, degree = buoy_ref.shape
    modal = []
    for field, coeff_ref in enumerate((buoy_ref, vel_ref)):
        parts = []
        for ref in in_refs:
            part = ref[:, field]
            parts.append(part.reshape(part.shape[0] * part.shape[1], span, lanes))
        fluxes = jnp.concatenate(parts, axis=0).astype(F32)
        fluxes = jnp.swapaxes(fluxes, 0, 1).astype(BF16)
        rows = []
        for mode in range(span):
            tend = lax.dot_general(
                fluxes[mode], proj_ref[...], (((0,), (0,)), ((), ())), preferred_element_type=F32
            )
            rows.append((coeff_ref[mode].astype(F32) + explicit_step * tend).astype(BF16))
        modal.append(
            jnp.dot(jnp.concatenate(rows, axis=0), left_ref[...], preferred_element_type=F32)
        )
    first = pl.program_id(0) * span
    waves = [4.0 * (wave_x_ref[first + mode] + wave_y_ref[...]) for mode in range(span)]
    solved = solve_modal(modal[0], modal[1], jnp.concatenate(waves, axis=0), eig_val_ref[...])
    for values, out_ref in zip(solved, out_refs):
        result = jnp.dot(values, right_ref[...], preferred_element_type=F32).astype(BF16)
        out_ref[...] = result.reshape(span, lanes, degree)


def finish(kernels, folded, buoy, vel_w, projs, eig_val, eig_left, eig_right, wave_x, wave_y):
    modes_x, modes_y, degree = buoy.shape
    if not kernels:
        tend = 0.0
        for part, proj in zip(folded, projs):
            parts = jnp.transpose(part, (1, 0, 2, 3, 4)).reshape(2, -1, modes_x, modes_y)
            tend += jnp.einsum("fzak,zn->fakn", parts, proj, preferred_element_type=F32)
        modal = []
        for field, coeffs in enumerate((buoy, vel_w)):
            rhs = (coeffs.astype(F32) + explicit_step * tend[field]).astype(BF16)
            modal.append(jnp.einsum("akn,nj->akj", rhs, eig_left, preferred_element_type=F32))
        wave = 4.0 * (wave_x[:, None, None] + wave_y[None, :, None])
        solved = solve_modal(modal[0], modal[1], wave, eig_val)
        return tuple(
            jnp.einsum("akj,jn->akn", values, eig_right, preferred_element_type=F32).astype(BF16)
            for values in solved
        )
    span = 8
    proj = jnp.concatenate(projs, axis=0)
    field_block = pl.BlockSpec((span, modes_y, degree), lambda a: (a, 0, 0))
    result = jax.ShapeDtypeStruct(buoy.shape, BF16)
    return pl.pallas_call(
        finish_kernel,
        grid=(modes_x // span,),
        in_specs=[
            pl.BlockSpec(memory_space=pltpu.SMEM),
            whole((modes_y, 1)),
            whole((1, degree)),
            whole(eig_left.shape),
            whole(eig_right.shape),
            whole(proj.shape),
            field_block,
            field_block,
        ]
        + [
            pl.BlockSpec(
                (part.shape[0], 2, part.shape[2], span, modes_y), lambda a: (0, 0, 0, a, 0)
            )
            for part in folded
        ],
        out_specs=[field_block, field_block],
        out_shape=[result, result],
        compiler_params=params(1),
        cost_estimate=pl.CostEstimate(
            flops=4 * buoy.size * (proj.shape[0] + 2 * degree),
            bytes_accessed=8 * buoy.size + sum(2 * part.size for part in folded),
            transcendentals=buoy.size,
        ),
        name="finish",
    )(
        wave_x,
        wave_y[:, None],
        eig_val[None, :],
        eig_left,
        eig_right,
        proj,
        buoy,
        vel_w,
        *folded,
    )


def chunk_sizes(own):
    first = min(own, max(1, own * 4 // 18))
    second = (own - first) // 2
    return [size for size in (first, second, own - first - second) if size]


def per_device(buoy, vel_w, strat, eig_val, eig_left, eig_right):
    row_count = lax.axis_size("row")
    col_count = lax.axis_size("col")
    blocks = row_count * col_count
    modes_x, modes_y, degree = buoy.shape
    total_x, total_y = modes_x * row_count, modes_y * col_count
    grid_x, grid_y = 3 * total_x // 2, 3 * total_y // 2
    shard = strat.shape[0]
    own = -(-shard // row_count)
    padding = own * row_count - shard
    kernels = modes_y % 128 == 0 and modes_x % 16 == 0 and degree % 128 == 0
    row = lax.axis_index("row")
    col = lax.axis_index("col")


    def by_device(table):
        table = table.reshape(col_count, shard, degree)
        table = np.pad(table, ((0, 0), (0, padding), (0, 0)))
        table = table.reshape(col_count, row_count, own, degree)
        return np.transpose(table, (1, 0, 2, 3)).reshape(blocks, own, degree)

    def exchange(values):
        return lax.all_to_all(values, ("row", "col"), split_axis=0, concat_axis=0, tiled=True)

    levels, slopes, projector = cheb_tables(degree, shard * col_count)
    forward_z = np.stack([by_device(levels.T), by_device(slopes.T)])
    backward_z = by_device(projector)
    along_x = jnp.asarray(np.ascontiguousarray(fourier_eval(total_x, grid_x).T))
    back_x = jnp.asarray(np.ascontiguousarray(fourier_proj(total_x, grid_x).T))
    along_y = jnp.asarray(fourier_eval(total_y, grid_y))
    back_y = jnp.asarray(np.ascontiguousarray(fourier_proj(total_y, grid_y)))
    strat_own = lax.dynamic_slice_in_dim(jnp.pad(strat, (0, padding)), row * own, own)

    folded, projs = [], []
    start = 0
    for depth in chunk_sizes(own):
        stop = start + depth
        table = jnp.asarray(forward_z[:, :, start:stop].reshape(2, blocks * depth, degree))
        projs.append(jnp.asarray(backward_z[:, start:stop].reshape(blocks * depth, degree)))
        arrived = exchange(lift(kernels, vel_w, buoy, table, blocks))
        fluxes = planes(
            kernels,
            arrived,
            strat_own[start:stop],
            along_y,
            along_x,
            back_x,
            back_y,
            col_count,
        )
        folded.append(exchange(fluxes))
        start = stop
    wave_x = wave_squares(total_x, row * modes_x, modes_x)
    wave_y = wave_squares(total_y, col * modes_y, modes_y)
    return finish(
        kernels, folded, buoy, vel_w, projs, eig_val, eig_left, eig_right, wave_x, wave_y
    )


def solution(mesh):
    in_specs = (P("row", "col", None), P("row", "col", None), P("col"), P(), P(), P())
    out_specs = (P("row", "col", None), P("row", "col", None))
    return jax.shard_map(
        per_device, mesh=mesh, in_specs=in_specs, out_specs=out_specs, check_vma=False
    )
```

```python
import math

import jax
import jax.numpy as jnp
import numpy as np
from jax import lax
from jax.experimental import pallas as pl
from jax.experimental.pallas import tpu as pltpu
from jax.sharding import PartitionSpec as P

explicit_step = 0.5
diffuse_buoy = 0.5
diffuse_vel = 0.25
couple_buoy = 0.7
couple_vel = 0.7

BF16 = jnp.bfloat16
F32 = jnp.float32
VMEM_BYTES = 56 * 1024 * 1024


def fourier_trig(modes, points):
    order = np.arange(modes, dtype=np.int32)
    freq = ((order + 1) // 2).astype(np.float32)
    place = np.arange(points, dtype=np.float32)
    angle = np.float32(2.0 * math.pi / points) * freq[:, None] * place[None, :]
    return (order, np.where((order % 2 == 0)[:, None], np.cos(angle), np.sin(angle)))


def fourier_eval(modes, points):
    order, values = fourier_trig(modes, points)
    return (values * np.float32(math.sqrt(2.0 / modes))).astype(BF16)


def fourier_proj(modes, points):
    order, values = fourier_trig(modes, points)
    weight = np.where(order == 0, 1.0 / points, 2.0 / points).astype(np.float32)
    return np.transpose(values * weight[:, None] * np.float32(math.sqrt(modes / 2.0))).astype(BF16)


def cheb_tables(degree, points):
    order = np.arange(degree, dtype=np.float32)
    theta = np.float32(math.pi) * (np.arange(points, dtype=np.float32) + np.float32(0.5)) / np.float32(points)
    angle = order[:, None] * theta[None, :]
    norm = np.float32(math.sqrt(2.0 / degree))
    levels = np.cos(angle) * norm
    slopes = -(order[:, None] / np.float32(degree)) * np.sin(angle) * norm
    weight = np.where(order == 0, 1.0 / points, 2.0 / points).astype(np.float32)
    projector = np.transpose(np.cos(angle) * weight[:, None] * np.float32(math.sqrt(degree / 2.0)))
    return (levels.astype(BF16), slopes.astype(BF16), projector.astype(BF16))


def wave_squares(modes, offset, count):
    order = offset + jnp.arange(count, dtype=jnp.int32)
    freq = ((order + 1) // 2).astype(F32) * (2.0 / modes)
    return freq * freq


def params(grid_rank):
    return pltpu.CompilerParams(
        dimension_semantics=("arbitrary",) * grid_rank, vmem_limit_bytes=VMEM_BYTES
    )


def whole(shape):
    return pl.BlockSpec(shape, lambda *_: (0,) * len(shape))


def lift_kernel(vel_ref, buoy_ref, table_ref, out_ref):
    blocks, fields, depth, span, lanes = out_ref.shape
    for field, source in enumerate((vel_ref, buoy_ref)):
        coeffs = source[...].reshape(span * lanes, source.shape[-1])
        values = lax.dot_general(
            table_ref[field], coeffs, (((1,), (1,)), ((), ())), preferred_element_type=F32
        )
        values = values.reshape(blocks * depth, span, lanes).astype(BF16)
        out_ref[:, field] = values.reshape(blocks, depth, span, lanes)


def lift(kernels, vel_w, buoy, table, blocks):
    modes_x, modes_y, degree = vel_w.shape
    depth = table.shape[1] // blocks
    shape = (blocks, 2, depth, modes_x, modes_y)
    if not kernels:
        fields = jnp.stack([vel_w, buoy])
        values = jnp.einsum("fzn,fakn->fzak", table, fields, preferred_element_type=F32)
        values = values.astype(BF16).reshape(2, blocks, depth, modes_x, modes_y)
        return jnp.transpose(values, (1, 0, 2, 3, 4))
    span = 16
    return pl.pallas_call(
        lift_kernel,
        grid=(modes_x // span,),
        in_specs=[
            pl.BlockSpec((span, modes_y, degree), lambda a: (a, 0, 0)),
            pl.BlockSpec((span, modes_y, degree), lambda a: (a, 0, 0)),
            whole(table.shape),
        ],
        out_specs=pl.BlockSpec((blocks, 2, depth, span, modes_y), lambda a: (0, 0, 0, a, 0)),
        out_shape=jax.ShapeDtypeStruct(shape, BF16),
        compiler_params=params(1),
        cost_estimate=pl.CostEstimate(
            flops=2 * math.prod(shape) * degree,
            bytes_accessed=2 * (2 * vel_w.size + math.prod(shape)),
            transcendentals=0,
        ),
        name="lift",
    )(vel_w, buoy, table)


def plane_kernel(
    col_count, strat_ref, along_y_ref, along_x_ref, back_x_ref, back_y_ref, in_ref, *refs
):
    out_ref = refs[-1]
    blocks, _, depth, modes_x, lanes = in_ref.shape
    row_count = blocks // col_count
    for level in range(depth):
        grids = []
        for field in range(2):
            rows = []
            for row in range(row_count):
                parts = [in_ref[row * col_count + col, field, level] for col in range(col_count)]
                rows.append(jnp.concatenate(parts, axis=1))
            middle = jnp.dot(
                jnp.concatenate(rows, axis=0), along_y_ref[...], preferred_element_type=F32
            ).astype(BF16)
            grid = jnp.dot(along_x_ref[...], middle, preferred_element_type=F32)
            grids.append(grid.astype(BF16).astype(F32))
        velocity, gradient = grids
        strata = strat_ref[pl.program_id(0) * depth + level]
        flux_buoy = (-(velocity * gradient) - strata * velocity).astype(BF16)
        flux_vel = (-(velocity * jnp.abs(velocity))).astype(BF16)
        for field, flux in enumerate((flux_buoy, flux_vel)):
            folded = jnp.dot(back_x_ref[...], flux, preferred_element_type=F32).astype(BF16)
            values = jnp.dot(folded, back_y_ref[...], preferred_element_type=F32).astype(BF16)
            for row in range(row_count):
                for col in range(col_count):
                    out_ref[row * col_count + col, field, level] = values[
                        row * modes_x : (row + 1) * modes_x, col * lanes : (col + 1) * lanes
                    ]


def planes(kernels, arrived, strat, along_y, along_x, back_x, back_y, col_count, after):
    blocks, fields, depth, modes_x, modes_y = arrived.shape
    row_count = blocks // col_count
    if not kernels:
        parts = arrived.reshape(row_count, col_count, fields, depth, modes_x, modes_y)
        parts = jnp.transpose(parts, (2, 3, 0, 4, 1, 5))
        parts = parts.reshape(fields, depth, row_count * modes_x, col_count * modes_y)
        middle = jnp.einsum("fzak,ky->fzay", parts, along_y, preferred_element_type=F32)
        grids = jnp.einsum("xa,fzay->fzxy", along_x, middle.astype(BF16), preferred_element_type=F32)
        grids = grids.astype(BF16).astype(F32)
        flux_buoy = -(grids[0] * grids[1]) - strat[:, None, None] * grids[0]
        flux_vel = -(grids[0] * jnp.abs(grids[0]))
        fluxes = jnp.stack([flux_buoy, flux_vel]).astype(BF16)
        folded = jnp.einsum("ax,fzxy->fzay", back_x, fluxes, preferred_element_type=F32)
        values = jnp.einsum("fzay,yk->fzak", folded.astype(BF16), back_y, preferred_element_type=F32)
        values = values.astype(BF16).reshape(
            fields, depth, row_count, modes_x, col_count, modes_y
        )
        return jnp.transpose(values, (2, 4, 0, 1, 3, 5)).reshape(arrived.shape)
    block = pl.BlockSpec((blocks, fields, 1, modes_x, modes_y), lambda z: (0, 0, z, 0, 0))
    work = along_y.size * along_x.shape[1] + along_x.size * along_y.shape[1]
    return pl.pallas_call(
        lambda *refs: plane_kernel(col_count, *refs),
        grid=(depth,),
        in_specs=[
            pl.BlockSpec(memory_space=pltpu.SMEM),
            whole(along_y.shape),
            whole(along_x.shape),
            whole(back_x.shape),
            whole(back_y.shape),
            block,
        ]
        + [pl.BlockSpec(memory_space=pl.ANY)] * len(after),
        out_specs=block,
        out_shape=jax.ShapeDtypeStruct(arrived.shape, BF16),
        compiler_params=params(1),
        cost_estimate=pl.CostEstimate(
            flops=4 * fields * depth * work, bytes_accessed=4 * arrived.size, transcendentals=0
        ),
        name="planes",
    )(strat, along_y, along_x, back_x, back_y, arrived, *after)


def solve_modal(modal_buoy, modal_vel, wave, eig_val):
    lapl = wave + eig_val
    diag_buoy = 1.0 + diffuse_buoy * lapl
    diag_vel = 1.0 + diffuse_vel * lapl
    scale = 1.0 / (diag_buoy * diag_vel + couple_buoy * couple_vel)
    solved_buoy = ((diag_vel * modal_buoy - couple_buoy * modal_vel) * scale).astype(BF16)
    solved_vel = ((diag_buoy * modal_vel + couple_vel * modal_buoy) * scale).astype(BF16)
    return (solved_buoy, solved_vel)


def project(ref, field, proj_ref):
    blocks, _, depth, span, lanes = ref.shape
    fluxes = ref[:, field].reshape(blocks * depth, span, lanes).astype(F32)
    fluxes = jnp.swapaxes(fluxes, 0, 1).astype(BF16)
    rows = [jnp.transpose(fluxes[mode]) for mode in range(span)]
    return jnp.dot(jnp.concatenate(rows, axis=0), proj_ref[...], preferred_element_type=F32)


def gather_kernel(proj_ref, buoy_ref, vel_ref, in_ref, *out_refs):
    span, lanes, degree = buoy_ref.shape
    for field, (coeff_ref, out_ref) in enumerate(zip((buoy_ref, vel_ref), out_refs)):
        tend = explicit_step * project(in_ref, field, proj_ref)
        out_ref[...] = coeff_ref[...].astype(F32) + tend.reshape(span, lanes, degree)


def gather(kernels, folded, proj, rhs):
    modes_x, modes_y, degree = rhs[0].shape
    blocks, fields, depth = folded.shape[:3]
    if not kernels:
        parts = jnp.transpose(folded, (1, 0, 2, 3, 4)).reshape(2, -1, modes_x, modes_y)
        tend = jnp.einsum("fzak,zn->fakn", parts, proj, preferred_element_type=F32)
        return [part.astype(F32) + explicit_step * tend[f] for f, part in enumerate(rhs)]
    span = 8
    block = pl.BlockSpec((span, modes_y, degree), lambda a: (a, 0, 0))
    return pl.pallas_call(
        gather_kernel,
        grid=(modes_x // span,),
        in_specs=[
            whole(proj.shape),
            block,
            block,
            pl.BlockSpec((blocks, fields, depth, span, modes_y), lambda a: (0, 0, 0, a, 0)),
        ],
        out_specs=[block, block],
        out_shape=[jax.ShapeDtypeStruct(rhs[0].shape, F32)] * 2,
        compiler_params=params(1),
        cost_estimate=pl.CostEstimate(
            flops=4 * rhs[0].size * proj.shape[0],
            bytes_accessed=2 * folded.size + 14 * rhs[0].size,
            transcendentals=0,
        ),
        name="gather",
    )(proj, *rhs, folded)


def finish_kernel(
    wave_x_ref,
    wave_y_ref,
    eig_val_ref,
    left_ref,
    right_ref,
    proj_ref,
    buoy_ref,
    vel_ref,
    in_ref,
    *out_refs,
):
    span, lanes, degree = buoy_ref.shape
    modal = []
    for field, rhs_ref in enumerate((buoy_ref, vel_ref)):
        tend = explicit_step * project(in_ref, field, proj_ref)
        rhs = rhs_ref[...].reshape(span * lanes, degree).astype(F32) + tend
        modal.append(jnp.dot(rhs.astype(BF16), left_ref[...], preferred_element_type=F32))
    first = pl.program_id(0) * span
    waves = [4.0 * (wave_x_ref[first + mode] + wave_y_ref[...]) for mode in range(span)]
    solved = solve_modal(modal[0], modal[1], jnp.concatenate(waves, axis=0), eig_val_ref[...])
    for values, out_ref in zip(solved, out_refs):
        result = jnp.dot(values, right_ref[...], preferred_element_type=F32).astype(BF16)
        out_ref[...] = result.reshape(span, lanes, degree)


def finish(kernels, folded, proj, rhs, eig_val, eig_left, eig_right, wave_x, wave_y):
    modes_x, modes_y, degree = rhs[0].shape
    if not kernels:
        modal = []
        for part in gather(kernels, folded, proj, rhs):
            part = part.astype(BF16)
            modal.append(jnp.einsum("akn,nj->akj", part, eig_left, preferred_element_type=F32))
        wave = 4.0 * (wave_x[:, None, None] + wave_y[None, :, None])
        solved = solve_modal(modal[0], modal[1], wave, eig_val)
        return tuple(
            jnp.einsum("akj,jn->akn", values, eig_right, preferred_element_type=F32).astype(BF16)
            for values in solved
        )
    span = 8
    blocks, fields, depth = folded.shape[:3]
    block = pl.BlockSpec((span, modes_y, degree), lambda a: (a, 0, 0))
    result = jax.ShapeDtypeStruct(rhs[0].shape, BF16)
    return pl.pallas_call(
        finish_kernel,
        grid=(modes_x // span,),
        in_specs=[
            pl.BlockSpec(memory_space=pltpu.SMEM),
            whole((modes_y, 1)),
            whole((1, degree)),
            whole(eig_left.shape),
            whole(eig_right.shape),
            whole(proj.shape),
            block,
            block,
            pl.BlockSpec((blocks, fields, depth, span, modes_y), lambda a: (0, 0, 0, a, 0)),
        ],
        out_specs=[block, block],
        out_shape=[result, result],
        compiler_params=params(1),
        cost_estimate=pl.CostEstimate(
            flops=4 * rhs[0].size * (proj.shape[0] + 2 * degree),
            bytes_accessed=12 * rhs[0].size + 2 * folded.size,
            transcendentals=rhs[0].size,
        ),
        name="finish",
    )(
        wave_x,
        wave_y[:, None],
        eig_val[None, :],
        eig_left,
        eig_right,
        proj,
        *rhs,
        folded,
    )


def chunk_sizes(own):
    first = min(own, max(1, own * 4 // 18))
    second = (own - first) // 2
    return [size for size in (first, second, own - first - second) if size]


def per_device(buoy, vel_w, strat, eig_val, eig_left, eig_right):
    row_count = lax.axis_size("row")
    col_count = lax.axis_size("col")
    blocks = row_count * col_count
    modes_x, modes_y, degree = buoy.shape
    total_x, total_y = modes_x * row_count, modes_y * col_count
    grid_x, grid_y = 3 * total_x // 2, 3 * total_y // 2
    shard = strat.shape[0]
    own = -(-shard // row_count)
    padding = own * row_count - shard
    kernels = modes_y % 128 == 0 and modes_x % 16 == 0 and degree % 128 == 0
    row = lax.axis_index("row")
    col = lax.axis_index("col")


    def by_device(table):
        table = table.reshape(col_count, shard, degree)
        table = np.pad(table, ((0, 0), (0, padding), (0, 0)))
        table = table.reshape(col_count, row_count, own, degree)
        return np.transpose(table, (1, 0, 2, 3)).reshape(blocks, own, degree)

    def exchange(values):
        return lax.all_to_all(values, ("row", "col"), split_axis=0, concat_axis=0, tiled=True)

    levels, slopes, projector = cheb_tables(degree, shard * col_count)
    forward_z = np.stack([by_device(levels.T), by_device(slopes.T)])
    backward_z = by_device(projector)
    along_x = jnp.asarray(np.ascontiguousarray(fourier_eval(total_x, grid_x).T))
    back_x = jnp.asarray(np.ascontiguousarray(fourier_proj(total_x, grid_x).T))
    along_y = jnp.asarray(fourier_eval(total_y, grid_y))
    back_y = jnp.asarray(np.ascontiguousarray(fourier_proj(total_y, grid_y)))
    strat_own = lax.dynamic_slice_in_dim(jnp.pad(strat, (0, padding)), row * own, own)

    sizes = chunk_sizes(own)
    stops = np.cumsum(sizes)
    pieces = [(int(stop - size), int(stop)) for size, stop in zip(sizes, stops)]
    arrived = []
    for start, stop in pieces:
        table = forward_z[:, :, start:stop].reshape(2, blocks * (stop - start), degree)
        arrived.append(exchange(lift(kernels, vel_w, buoy, jnp.asarray(table), blocks)))
    order = list(range(1, len(pieces))) + [0]
    folded, after = [], []
    for piece in order:
        start, stop = pieces[piece]
        fluxes = planes(
            kernels,
            arrived[piece],
            strat_own[start:stop],
            along_y,
            along_x,
            back_x,
            back_y,
            col_count,
            after,
        )
        after = [fluxes]
        folded.append(exchange(fluxes))
    projs = [
        jnp.asarray(backward_z[:, start:stop].reshape(blocks * (stop - start), degree))
        for start, stop in (pieces[piece] for piece in order)
    ]
    rhs = [buoy, vel_w]
    for part, proj in zip(folded[:-1], projs[:-1]):
        rhs = gather(kernels, part, proj, rhs)
    wave_x = wave_squares(total_x, row * modes_x, modes_x)
    wave_y = wave_squares(total_y, col * modes_y, modes_y)
    return finish(
        kernels, folded[-1], projs[-1], rhs, eig_val, eig_left, eig_right, wave_x, wave_y
    )


def solution(mesh):
    in_specs = (P("row", "col", None), P("row", "col", None), P("col"), P(), P(), P())
    out_specs = (P("row", "col", None), P("row", "col", None))
    return jax.shard_map(
        per_device, mesh=mesh, in_specs=in_specs, out_specs=out_specs, check_vma=False
    )
```

```python
import math

import jax
import jax.numpy as jnp
import numpy as np
from jax import lax
from jax.experimental import pallas as pl
from jax.experimental.pallas import tpu as pltpu
from jax.sharding import PartitionSpec as P

explicit_step = 0.5
diffuse_buoy = 0.5
diffuse_vel = 0.25
couple_buoy = 0.7
couple_vel = 0.7

BF16 = jnp.bfloat16
F32 = jnp.float32
VMEM_BYTES = 56 * 1024 * 1024


def fourier_trig(modes, points):
    order = np.arange(modes, dtype=np.int32)
    freq = ((order + 1) // 2).astype(np.float32)
    place = np.arange(points, dtype=np.float32)
    angle = np.float32(2.0 * math.pi / points) * freq[:, None] * place[None, :]
    return (order, np.where((order % 2 == 0)[:, None], np.cos(angle), np.sin(angle)))


def fourier_eval(modes, points):
    order, values = fourier_trig(modes, points)
    return (values * np.float32(math.sqrt(2.0 / modes))).astype(BF16)


def fourier_proj(modes, points):
    order, values = fourier_trig(modes, points)
    weight = np.where(order == 0, 1.0 / points, 2.0 / points).astype(np.float32)
    return np.transpose(values * weight[:, None] * np.float32(math.sqrt(modes / 2.0))).astype(BF16)


def cheb_tables(degree, points):
    order = np.arange(degree, dtype=np.float32)
    theta = np.float32(math.pi) * (np.arange(points, dtype=np.float32) + np.float32(0.5)) / np.float32(points)
    angle = order[:, None] * theta[None, :]
    norm = np.float32(math.sqrt(2.0 / degree))
    levels = np.cos(angle) * norm
    slopes = -(order[:, None] / np.float32(degree)) * np.sin(angle) * norm
    weight = np.where(order == 0, 1.0 / points, 2.0 / points).astype(np.float32)
    projector = np.transpose(np.cos(angle) * weight[:, None] * np.float32(math.sqrt(degree / 2.0)))
    return (levels.astype(BF16), slopes.astype(BF16), projector.astype(BF16))


def wave_squares(modes, offset, count):
    order = offset + jnp.arange(count, dtype=jnp.int32)
    freq = ((order + 1) // 2).astype(F32) * (2.0 / modes)
    return freq * freq


def params(grid_rank):
    return pltpu.CompilerParams(
        dimension_semantics=("arbitrary",) * grid_rank, vmem_limit_bytes=VMEM_BYTES
    )


def whole(shape):
    return pl.BlockSpec(shape, lambda *_: (0,) * len(shape))


def lift_kernel(vel_ref, buoy_ref, table_ref, out_ref):
    blocks, fields, depth, span, lanes = out_ref.shape
    for field, source in enumerate((vel_ref, buoy_ref)):
        coeffs = source[...].reshape(span * lanes, source.shape[-1])
        values = lax.dot_general(
            table_ref[field], coeffs, (((1,), (1,)), ((), ())), preferred_element_type=F32
        )
        values = values.reshape(blocks * depth, span, lanes).astype(BF16)
        out_ref[:, field] = values.reshape(blocks, depth, span, lanes)


def lift(kernels, vel_w, buoy, table, blocks):
    modes_x, modes_y, degree = vel_w.shape
    depth = table.shape[1] // blocks
    shape = (blocks, 2, depth, modes_x, modes_y)
    if not kernels:
        fields = jnp.stack([vel_w, buoy])
        values = jnp.einsum("fzn,fakn->fzak", table, fields, preferred_element_type=F32)
        values = values.astype(BF16).reshape(2, blocks, depth, modes_x, modes_y)
        return jnp.transpose(values, (1, 0, 2, 3, 4))
    span = 8
    return pl.pallas_call(
        lift_kernel,
        grid=(modes_x // span,),
        in_specs=[
            pl.BlockSpec((span, modes_y, degree), lambda a: (a, 0, 0)),
            pl.BlockSpec((span, modes_y, degree), lambda a: (a, 0, 0)),
            whole(table.shape),
        ],
        out_specs=pl.BlockSpec((blocks, 2, depth, span, modes_y), lambda a: (0, 0, 0, a, 0)),
        out_shape=jax.ShapeDtypeStruct(shape, BF16),
        compiler_params=params(1),
        cost_estimate=pl.CostEstimate(
            flops=2 * math.prod(shape) * degree,
            bytes_accessed=2 * (2 * vel_w.size + math.prod(shape)),
            transcendentals=0,
        ),
        name="lift",
    )(vel_w, buoy, table)


def plane_kernel(
    col_count, strat_ref, along_y_ref, along_x_ref, back_x_ref, back_y_ref, in_ref, *refs
):
    out_ref = refs[-1]
    blocks, _, depth, modes_x, lanes = in_ref.shape
    row_count = blocks // col_count
    for level in range(depth):
        grids = []
        for field in range(2):
            rows = []
            for row in range(row_count):
                parts = [in_ref[row * col_count + col, field, level] for col in range(col_count)]
                rows.append(jnp.concatenate(parts, axis=1))
            middle = jnp.dot(
                jnp.concatenate(rows, axis=0), along_y_ref[...], preferred_element_type=F32
            ).astype(BF16)
            grid = jnp.dot(along_x_ref[...], middle, preferred_element_type=F32)
            grids.append(grid.astype(BF16).astype(F32))
        velocity, gradient = grids
        strata = strat_ref[pl.program_id(0) * depth + level]
        flux_buoy = (-(velocity * gradient) - strata * velocity).astype(BF16)
        flux_vel = (-(velocity * jnp.abs(velocity))).astype(BF16)
        for field, flux in enumerate((flux_buoy, flux_vel)):
            folded = jnp.dot(back_x_ref[...], flux, preferred_element_type=F32).astype(BF16)
            values = jnp.dot(folded, back_y_ref[...], preferred_element_type=F32).astype(BF16)
            for row in range(row_count):
                for col in range(col_count):
                    out_ref[row * col_count + col, field, level] = values[
                        row * modes_x : (row + 1) * modes_x, col * lanes : (col + 1) * lanes
                    ]


def planes(kernels, arrived, strat, along_y, along_x, back_x, back_y, col_count, after):
    blocks, fields, depth, modes_x, modes_y = arrived.shape
    row_count = blocks // col_count
    if not kernels:
        parts = arrived.reshape(row_count, col_count, fields, depth, modes_x, modes_y)
        parts = jnp.transpose(parts, (2, 3, 0, 4, 1, 5))
        parts = parts.reshape(fields, depth, row_count * modes_x, col_count * modes_y)
        middle = jnp.einsum("fzak,ky->fzay", parts, along_y, preferred_element_type=F32)
        grids = jnp.einsum("xa,fzay->fzxy", along_x, middle.astype(BF16), preferred_element_type=F32)
        grids = grids.astype(BF16).astype(F32)
        flux_buoy = -(grids[0] * grids[1]) - strat[:, None, None] * grids[0]
        flux_vel = -(grids[0] * jnp.abs(grids[0]))
        fluxes = jnp.stack([flux_buoy, flux_vel]).astype(BF16)
        folded = jnp.einsum("ax,fzxy->fzay", back_x, fluxes, preferred_element_type=F32)
        values = jnp.einsum("fzay,yk->fzak", folded.astype(BF16), back_y, preferred_element_type=F32)
        values = values.astype(BF16).reshape(
            fields, depth, row_count, modes_x, col_count, modes_y
        )
        return jnp.transpose(values, (2, 4, 0, 1, 3, 5)).reshape(arrived.shape)
    block = pl.BlockSpec((blocks, fields, 1, modes_x, modes_y), lambda z: (0, 0, z, 0, 0))
    work = along_y.size * along_x.shape[1] + along_x.size * along_y.shape[1]
    return pl.pallas_call(
        lambda *refs: plane_kernel(col_count, *refs),
        grid=(depth,),
        in_specs=[
            pl.BlockSpec(memory_space=pltpu.SMEM),
            whole(along_y.shape),
            whole(along_x.shape),
            whole(back_x.shape),
            whole(back_y.shape),
            block,
        ]
        + [pl.BlockSpec(memory_space=pl.ANY)] * len(after),
        out_specs=block,
        out_shape=jax.ShapeDtypeStruct(arrived.shape, BF16),
        compiler_params=params(1),
        cost_estimate=pl.CostEstimate(
            flops=4 * fields * depth * work, bytes_accessed=4 * arrived.size, transcendentals=0
        ),
        name="planes",
    )(strat, along_y, along_x, back_x, back_y, arrived, *after)


def solve_modal(modal_buoy, modal_vel, wave, eig_val):
    diag_buoy = (1.0 + diffuse_buoy * wave) + diffuse_buoy * eig_val
    diag_vel = (1.0 + diffuse_vel * wave) + diffuse_vel * eig_val
    scale = 1.0 / (diag_buoy * diag_vel + couple_buoy * couple_vel)
    modal_buoy = modal_buoy * scale
    modal_vel = modal_vel * scale
    solved_buoy = (diag_vel * modal_buoy - couple_buoy * modal_vel).astype(BF16)
    solved_vel = (diag_buoy * modal_vel + couple_vel * modal_buoy).astype(BF16)
    return (solved_buoy, solved_vel)


def project(ref, field, proj_ref):
    blocks, _, depth, span, lanes = ref.shape
    fluxes = ref[:, field].reshape(blocks * depth, span, lanes).astype(F32)
    fluxes = jnp.swapaxes(fluxes, 0, 1).astype(BF16)
    rows = [jnp.transpose(fluxes[mode]) for mode in range(span)]
    return jnp.dot(jnp.concatenate(rows, axis=0), proj_ref[...], preferred_element_type=F32)


def gather_kernel(proj_ref, left_ref, buoy_ref, vel_ref, in_ref, *out_refs):
    span, lanes, degree = buoy_ref.shape
    for field, (coeff_ref, out_ref) in enumerate(zip((buoy_ref, vel_ref), out_refs)):
        tend = explicit_step * project(in_ref, field, proj_ref)
        rhs = coeff_ref[...].reshape(span * lanes, degree).astype(F32) + tend
        modal = jnp.dot(rhs.astype(BF16), left_ref[...], preferred_element_type=F32)
        out_ref[...] = modal.reshape(span, lanes, degree)


def gather(kernels, folded, proj, eig_left, fields):
    modes_x, modes_y, degree = fields[0].shape
    blocks, count, depth = folded.shape[:3]
    if not kernels:
        parts = jnp.transpose(folded, (1, 0, 2, 3, 4)).reshape(2, -1, modes_x, modes_y)
        tend = jnp.einsum("fzak,zn->fakn", parts, proj, preferred_element_type=F32)
        rhs = jnp.stack(fields).astype(F32) + explicit_step * tend
        modal = jnp.einsum("fakn,nj->fakj", rhs.astype(BF16), eig_left, preferred_element_type=F32)
        return [modal[0], modal[1]]
    span = 8
    block = pl.BlockSpec((span, modes_y, degree), lambda a: (a, 0, 0))
    return pl.pallas_call(
        gather_kernel,
        grid=(modes_x // span,),
        in_specs=[
            whole(proj.shape),
            whole(eig_left.shape),
            block,
            block,
            pl.BlockSpec((blocks, count, depth, span, modes_y), lambda a: (0, 0, 0, a, 0)),
        ],
        out_specs=[block, block],
        out_shape=[jax.ShapeDtypeStruct(fields[0].shape, F32)] * 2,
        compiler_params=params(1),
        cost_estimate=pl.CostEstimate(
            flops=4 * fields[0].size * (proj.shape[0] + degree),
            bytes_accessed=2 * folded.size + 12 * fields[0].size,
            transcendentals=0,
        ),
        name="gather",
    )(proj, eig_left, *fields, folded)


def finish_kernel(
    wave_x_ref, wave_y_ref, eig_val_ref, right_ref, proj_ref, buoy_ref, vel_ref, in_ref, *out_refs
):
    span, lanes, degree = buoy_ref.shape
    modal = []
    for field, part_ref in enumerate((buoy_ref, vel_ref)):
        part = part_ref[...].reshape(span * lanes, degree)
        modal.append(part + project(in_ref, field, proj_ref))
    first = pl.program_id(0) * span
    waves = [4.0 * (wave_x_ref[first + mode] + wave_y_ref[...]) for mode in range(span)]
    solved = solve_modal(modal[0], modal[1], jnp.concatenate(waves, axis=0), eig_val_ref[...])
    for values, out_ref in zip(solved, out_refs):
        result = jnp.dot(values, right_ref[...], preferred_element_type=F32).astype(BF16)
        out_ref[...] = result.reshape(span, lanes, degree)


def finish(kernels, folded, proj, modal, eig_val, eig_right, wave_x, wave_y):
    modes_x, modes_y, degree = modal[0].shape
    if not kernels:
        parts = jnp.transpose(folded, (1, 0, 2, 3, 4)).reshape(2, -1, modes_x, modes_y)
        last = jnp.einsum("fzak,zn->fakn", parts, proj, preferred_element_type=F32)
        wave = 4.0 * (wave_x[:, None, None] + wave_y[None, :, None])
        solved = solve_modal(modal[0] + last[0], modal[1] + last[1], wave, eig_val)
        return tuple(
            jnp.einsum("akj,jn->akn", values, eig_right, preferred_element_type=F32).astype(BF16)
            for values in solved
        )
    span = 8
    blocks, fields, depth = folded.shape[:3]
    block = pl.BlockSpec((span, modes_y, degree), lambda a: (a, 0, 0))
    result = jax.ShapeDtypeStruct(modal[0].shape, BF16)
    return pl.pallas_call(
        finish_kernel,
        grid=(modes_x // span,),
        in_specs=[
            pl.BlockSpec(memory_space=pltpu.SMEM),
            whole((modes_y, 1)),
            whole((1, degree)),
            whole(eig_right.shape),
            whole(proj.shape),
            block,
            block,
            pl.BlockSpec((blocks, fields, depth, span, modes_y), lambda a: (0, 0, 0, a, 0)),
        ],
        out_specs=[block, block],
        out_shape=[result, result],
        compiler_params=params(1),
        cost_estimate=pl.CostEstimate(
            flops=4 * modal[0].size * (proj.shape[0] + degree),
            bytes_accessed=12 * modal[0].size + 2 * folded.size,
            transcendentals=modal[0].size,
        ),
        name="finish",
    )(wave_x, wave_y[:, None], eig_val[None, :], eig_right, proj, *modal, folded)


def chunk_sizes(own):
    second = -(-own * 4 // 18)
    return [size for size in (own - second, second) if size]


def per_device(buoy, vel_w, strat, eig_val, eig_left, eig_right):
    row_count = lax.axis_size("row")
    col_count = lax.axis_size("col")
    blocks = row_count * col_count
    modes_x, modes_y, degree = buoy.shape
    total_x, total_y = modes_x * row_count, modes_y * col_count
    grid_x, grid_y = 3 * total_x // 2, 3 * total_y // 2
    shard = strat.shape[0]
    own = -(-shard // row_count)
    padding = own * row_count - shard
    kernels = modes_y % 128 == 0 and modes_x % 16 == 0 and degree % 128 == 0
    row = lax.axis_index("row")
    col = lax.axis_index("col")


    def by_device(table):
        table = table.reshape(col_count, shard, degree)
        table = np.pad(table, ((0, 0), (0, padding), (0, 0)))
        table = table.reshape(col_count, row_count, own, degree)
        return np.transpose(table, (1, 0, 2, 3)).reshape(blocks, own, degree)

    def exchange(values):
        return lax.all_to_all(values, ("row", "col"), split_axis=0, concat_axis=0, tiled=True)

    levels, slopes, projector = cheb_tables(degree, shard * col_count)
    forward_z = np.stack([by_device(levels.T), by_device(slopes.T)])
    backward_z = by_device(projector)
    along_x = jnp.asarray(np.ascontiguousarray(fourier_eval(total_x, grid_x).T))
    back_x = jnp.asarray(np.ascontiguousarray(fourier_proj(total_x, grid_x).T))
    along_y = jnp.asarray(fourier_eval(total_y, grid_y))
    back_y = jnp.asarray(np.ascontiguousarray(fourier_proj(total_y, grid_y)))
    strat_own = lax.dynamic_slice_in_dim(jnp.pad(strat, (0, padding)), row * own, own)

    sizes = chunk_sizes(own)
    stops = np.cumsum(sizes)
    pieces = [(int(stop - size), int(stop)) for size, stop in zip(sizes, stops)]
    arrived = []
    for start, stop in pieces:
        table = forward_z[:, :, start:stop].reshape(2, blocks * (stop - start), degree)
        arrived.append(exchange(lift(kernels, vel_w, buoy, jnp.asarray(table), blocks)))
    folded, after = [], []
    for values, (start, stop) in zip(arrived, pieces):
        fluxes = planes(
            kernels,
            values,
            strat_own[start:stop],
            along_y,
            along_x,
            back_x,
            back_y,
            col_count,
            after,
        )
        after = [fluxes]
        folded.append(exchange(fluxes))
    projs = [
        jnp.asarray(backward_z[:, start:stop].reshape(blocks * (stop - start), degree))
        for start, stop in pieces
    ]
    if len(pieces) > 1:
        modal = gather(kernels, folded[0], projs[0], eig_left, [buoy, vel_w])
    else:
        modal = [
            jnp.einsum("akn,nj->akj", part, eig_left, preferred_element_type=F32)
            for part in (buoy, vel_w)
        ]
    last = jnp.dot(projs[-1], eig_left, preferred_element_type=F32)
    last = (explicit_step * last).astype(BF16)
    wave_x = wave_squares(total_x, row * modes_x, modes_x)
    wave_y = wave_squares(total_y, col * modes_y, modes_y)
    return finish(kernels, folded[-1], last, modal, eig_val, eig_right, wave_x, wave_y)


def solution(mesh):
    in_specs = (P("row", "col", None), P("row", "col", None), P("col"), P(), P(), P())
    out_specs = (P("row", "col", None), P("row", "col", None))
    return jax.shard_map(
        per_device, mesh=mesh, in_specs=in_specs, out_specs=out_specs, check_vma=False
    )
```

```python
import math

import jax
import jax.numpy as jnp
import numpy as np
from jax import lax
from jax.experimental import pallas as pl
from jax.experimental.pallas import tpu as pltpu
from jax.sharding import PartitionSpec as P

explicit_step = 0.5
diffuse_buoy = 0.5
diffuse_vel = 0.25
couple_buoy = 0.7
couple_vel = 0.7

BF16 = jnp.bfloat16
F32 = jnp.float32
VMEM_BYTES = 56 * 1024 * 1024


def fourier_trig(modes, points):
    order = np.arange(modes, dtype=np.int32)
    freq = ((order + 1) // 2).astype(np.float32)
    place = np.arange(points, dtype=np.float32)
    angle = np.float32(2.0 * math.pi / points) * freq[:, None] * place[None, :]
    return (order, np.where((order % 2 == 0)[:, None], np.cos(angle), np.sin(angle)))


def fourier_eval(modes, points):
    order, values = fourier_trig(modes, points)
    return (values * np.float32(math.sqrt(2.0 / modes))).astype(BF16)


def fourier_proj(modes, points):
    order, values = fourier_trig(modes, points)
    weight = np.where(order == 0, 1.0 / points, 2.0 / points).astype(np.float32)
    return np.transpose(values * weight[:, None] * np.float32(math.sqrt(modes / 2.0))).astype(BF16)


def cheb_tables(degree, points):
    order = np.arange(degree, dtype=np.float32)
    theta = np.float32(math.pi) * (np.arange(points, dtype=np.float32) + np.float32(0.5)) / np.float32(points)
    angle = order[:, None] * theta[None, :]
    norm = np.float32(math.sqrt(2.0 / degree))
    levels = np.cos(angle) * norm
    slopes = -(order[:, None] / np.float32(degree)) * np.sin(angle) * norm
    weight = np.where(order == 0, 1.0 / points, 2.0 / points).astype(np.float32)
    projector = np.transpose(np.cos(angle) * weight[:, None] * np.float32(math.sqrt(degree / 2.0)))
    return (levels.astype(BF16), slopes.astype(BF16), projector.astype(BF16))


def wave_squares(modes, offset, count):
    order = offset + jnp.arange(count, dtype=jnp.int32)
    freq = ((order + 1) // 2).astype(F32) * (2.0 / modes)
    return freq * freq


def params(grid_rank):
    return pltpu.CompilerParams(
        dimension_semantics=("arbitrary",) * grid_rank, vmem_limit_bytes=VMEM_BYTES
    )


def whole(shape):
    return pl.BlockSpec(shape, lambda *_: (0,) * len(shape))


def lift_kernel(vel_ref, buoy_ref, table_ref, out_ref):
    blocks, fields, depth, span, lanes = out_ref.shape
    for field, source in enumerate((vel_ref, buoy_ref)):
        coeffs = source[...].reshape(span * lanes, source.shape[-1])
        values = lax.dot_general(
            table_ref[field], coeffs, (((1,), (1,)), ((), ())), preferred_element_type=F32
        )
        values = values.reshape(blocks * depth, span, lanes).astype(BF16)
        out_ref[:, field] = values.reshape(blocks, depth, span, lanes)


def lift(kernels, vel_w, buoy, table, blocks):
    modes_x, modes_y, degree = vel_w.shape
    depth = table.shape[1] // blocks
    shape = (blocks, 2, depth, modes_x, modes_y)
    if not kernels:
        fields = jnp.stack([vel_w, buoy])
        values = jnp.einsum("fzn,fakn->fzak", table, fields, preferred_element_type=F32)
        values = values.astype(BF16).reshape(2, blocks, depth, modes_x, modes_y)
        return jnp.transpose(values, (1, 0, 2, 3, 4))
    span = 8
    return pl.pallas_call(
        lift_kernel,
        grid=(modes_x // span,),
        in_specs=[
            pl.BlockSpec((span, modes_y, degree), lambda a: (a, 0, 0)),
            pl.BlockSpec((span, modes_y, degree), lambda a: (a, 0, 0)),
            whole(table.shape),
        ],
        out_specs=pl.BlockSpec((blocks, 2, depth, span, modes_y), lambda a: (0, 0, 0, a, 0)),
        out_shape=jax.ShapeDtypeStruct(shape, BF16),
        compiler_params=params(1),
        cost_estimate=pl.CostEstimate(
            flops=2 * math.prod(shape) * degree,
            bytes_accessed=2 * (2 * vel_w.size + math.prod(shape)),
            transcendentals=0,
        ),
        name="lift",
    )(vel_w, buoy, table)


def plane_kernel(
    col_count, strat_ref, along_y_ref, along_x_ref, back_x_ref, back_y_ref, in_ref, *refs
):
    out_ref = refs[-1]
    blocks, _, depth, modes_x, lanes = in_ref.shape
    row_count = blocks // col_count
    for level in range(depth):
        grids = []
        for field in range(2):
            rows = []
            for row in range(row_count):
                parts = [in_ref[col * row_count + row, field, level] for col in range(col_count)]
                rows.append(jnp.concatenate(parts, axis=1))
            middle = jnp.dot(
                jnp.concatenate(rows, axis=0), along_y_ref[...], preferred_element_type=F32
            ).astype(BF16)
            grid = jnp.dot(along_x_ref[...], middle, preferred_element_type=F32)
            grids.append(grid.astype(BF16).astype(F32))
        velocity, gradient = grids
        strata = strat_ref[pl.program_id(0) * depth + level]
        flux_buoy = (-(velocity * gradient) - strata * velocity).astype(BF16)
        flux_vel = (-(velocity * jnp.abs(velocity))).astype(BF16)
        for field, flux in enumerate((flux_buoy, flux_vel)):
            folded = jnp.dot(back_x_ref[...], flux, preferred_element_type=F32).astype(BF16)
            values = jnp.dot(folded, back_y_ref[...], preferred_element_type=F32).astype(BF16)
            for row in range(row_count):
                for col in range(col_count):
                    out_ref[col * row_count + row, field, level] = values[
                        row * modes_x : (row + 1) * modes_x, col * lanes : (col + 1) * lanes
                    ]


def planes(kernels, arrived, strat, along_y, along_x, back_x, back_y, col_count, after):
    blocks, fields, depth, modes_x, modes_y = arrived.shape
    row_count = blocks // col_count
    if not kernels:
        parts = arrived.reshape(col_count, row_count, fields, depth, modes_x, modes_y)
        parts = jnp.transpose(parts, (2, 3, 1, 4, 0, 5))
        parts = parts.reshape(fields, depth, row_count * modes_x, col_count * modes_y)
        middle = jnp.einsum("fzak,ky->fzay", parts, along_y, preferred_element_type=F32)
        grids = jnp.einsum("xa,fzay->fzxy", along_x, middle.astype(BF16), preferred_element_type=F32)
        grids = grids.astype(BF16).astype(F32)
        flux_buoy = -(grids[0] * grids[1]) - strat[:, None, None] * grids[0]
        flux_vel = -(grids[0] * jnp.abs(grids[0]))
        fluxes = jnp.stack([flux_buoy, flux_vel]).astype(BF16)
        folded = jnp.einsum("ax,fzxy->fzay", back_x, fluxes, preferred_element_type=F32)
        values = jnp.einsum("fzay,yk->fzak", folded.astype(BF16), back_y, preferred_element_type=F32)
        values = values.astype(BF16).reshape(
            fields, depth, row_count, modes_x, col_count, modes_y
        )
        return jnp.transpose(values, (4, 2, 0, 1, 3, 5)).reshape(arrived.shape)
    block = pl.BlockSpec((blocks, fields, 1, modes_x, modes_y), lambda z: (0, 0, z, 0, 0))
    work = along_y.size * along_x.shape[1] + along_x.size * along_y.shape[1]
    return pl.pallas_call(
        lambda *refs: plane_kernel(col_count, *refs),
        grid=(depth,),
        in_specs=[
            pl.BlockSpec(memory_space=pltpu.SMEM),
            whole(along_y.shape),
            whole(along_x.shape),
            whole(back_x.shape),
            whole(back_y.shape),
            block,
        ]
        + [pl.BlockSpec(memory_space=pl.ANY)] * len(after),
        out_specs=block,
        out_shape=jax.ShapeDtypeStruct(arrived.shape, BF16),
        compiler_params=params(1),
        cost_estimate=pl.CostEstimate(
            flops=4 * fields * depth * work, bytes_accessed=4 * arrived.size, transcendentals=0
        ),
        name="planes",
    )(strat, along_y, along_x, back_x, back_y, arrived, *after)


def solve_modal(modal_buoy, modal_vel, wave, eig_val):
    diag_buoy = (1.0 + diffuse_buoy * wave) + diffuse_buoy * eig_val
    diag_vel = (1.0 + diffuse_vel * wave) + diffuse_vel * eig_val
    scale = 1.0 / (diag_buoy * diag_vel + couple_buoy * couple_vel)
    modal_buoy = modal_buoy * scale
    modal_vel = modal_vel * scale
    solved_buoy = (diag_vel * modal_buoy - couple_buoy * modal_vel).astype(BF16)
    solved_vel = (diag_buoy * modal_vel + couple_vel * modal_buoy).astype(BF16)
    return (solved_buoy, solved_vel)


def project(refs, field, proj_ref):
    blocks, _, _, span, lanes = refs[0].shape
    parts = [ref[:, field].reshape(blocks * ref.shape[2], span, lanes) for ref in refs]
    fluxes = jnp.concatenate(parts, axis=0).astype(F32)
    fluxes = jnp.swapaxes(fluxes, 0, 1).astype(BF16)
    rows = [jnp.transpose(fluxes[mode]) for mode in range(span)]
    return jnp.dot(jnp.concatenate(rows, axis=0), proj_ref[...], preferred_element_type=F32)


def gather_kernel(proj_ref, left_ref, buoy_ref, vel_ref, *refs):
    in_refs, out_refs = refs[:-2], refs[-2:]
    span, lanes, degree = buoy_ref.shape
    for field, (coeff_ref, out_ref) in enumerate(zip((buoy_ref, vel_ref), out_refs)):
        tend = explicit_step * project(in_refs, field, proj_ref)
        rhs = coeff_ref[...].reshape(span * lanes, degree).astype(F32) + tend
        modal = jnp.dot(rhs.astype(BF16), left_ref[...], preferred_element_type=F32)
        out_ref[...] = modal.reshape(span, lanes, degree)


def gather(kernels, folded, proj, eig_left, fields):
    modes_x, modes_y, degree = fields[0].shape
    if not kernels:
        parts = [
            jnp.transpose(part, (1, 0, 2, 3, 4)).reshape(2, -1, modes_x, modes_y)
            for part in folded
        ]
        parts = jnp.concatenate(parts, axis=1)
        tend = jnp.einsum("fzak,zn->fakn", parts, proj, preferred_element_type=F32)
        rhs = jnp.stack(fields).astype(F32) + explicit_step * tend
        modal = jnp.einsum("fakn,nj->fakj", rhs.astype(BF16), eig_left, preferred_element_type=F32)
        return [modal[0], modal[1]]
    span = 8
    block = pl.BlockSpec((span, modes_y, degree), lambda a: (a, 0, 0))
    return pl.pallas_call(
        gather_kernel,
        grid=(modes_x // span,),
        in_specs=[
            whole(proj.shape),
            whole(eig_left.shape),
            block,
            block,
        ]
        + [
            pl.BlockSpec((*part.shape[:3], span, modes_y), lambda a: (0, 0, 0, a, 0))
            for part in folded
        ],
        out_specs=[block, block],
        out_shape=[jax.ShapeDtypeStruct(fields[0].shape, F32)] * 2,
        compiler_params=params(1),
        cost_estimate=pl.CostEstimate(
            flops=4 * fields[0].size * (proj.shape[0] + degree),
            bytes_accessed=2 * sum(part.size for part in folded) + 12 * fields[0].size,
            transcendentals=0,
        ),
        name="gather",
    )(proj, eig_left, *fields, *folded)


def finish_kernel(
    wave_x_ref, wave_y_ref, eig_val_ref, right_ref, proj_ref, buoy_ref, vel_ref, in_ref, *out_refs
):
    span, lanes, degree = buoy_ref.shape
    modal = []
    for field, part_ref in enumerate((buoy_ref, vel_ref)):
        part = part_ref[...].reshape(span * lanes, degree)
        modal.append(part + project([in_ref], field, proj_ref))
    first = pl.program_id(0) * span
    waves = [4.0 * (wave_x_ref[first + mode] + wave_y_ref[...]) for mode in range(span)]
    solved = solve_modal(modal[0], modal[1], jnp.concatenate(waves, axis=0), eig_val_ref[...])
    for values, out_ref in zip(solved, out_refs):
        result = jnp.dot(values, right_ref[...], preferred_element_type=F32).astype(BF16)
        out_ref[...] = result.reshape(span, lanes, degree)


def finish(kernels, folded, proj, modal, eig_val, eig_right, wave_x, wave_y):
    modes_x, modes_y, degree = modal[0].shape
    if not kernels:
        parts = jnp.transpose(folded, (1, 0, 2, 3, 4)).reshape(2, -1, modes_x, modes_y)
        last = jnp.einsum("fzak,zn->fakn", parts, proj, preferred_element_type=F32)
        wave = 4.0 * (wave_x[:, None, None] + wave_y[None, :, None])
        solved = solve_modal(modal[0] + last[0], modal[1] + last[1], wave, eig_val)
        return tuple(
            jnp.einsum("akj,jn->akn", values, eig_right, preferred_element_type=F32).astype(BF16)
            for values in solved
        )
    span = 8
    blocks, fields, depth = folded.shape[:3]
    block = pl.BlockSpec((span, modes_y, degree), lambda a: (a, 0, 0))
    result = jax.ShapeDtypeStruct(modal[0].shape, BF16)
    return pl.pallas_call(
        finish_kernel,
        grid=(modes_x // span,),
        in_specs=[
            pl.BlockSpec(memory_space=pltpu.SMEM),
            whole((modes_y, 1)),
            whole((1, degree)),
            whole(eig_right.shape),
            whole(proj.shape),
            block,
            block,
            pl.BlockSpec((blocks, fields, depth, span, modes_y), lambda a: (0, 0, 0, a, 0)),
        ],
        out_specs=[block, block],
        out_shape=[result, result],
        compiler_params=params(1),
        cost_estimate=pl.CostEstimate(
            flops=4 * modal[0].size * (proj.shape[0] + degree),
            bytes_accessed=12 * modal[0].size + 2 * folded.size,
            transcendentals=modal[0].size,
        ),
        name="finish",
    )(wave_x, wave_y[:, None], eig_val[None, :], eig_right, proj, *modal, folded)


def chunk_sizes(own):
    first = -(-own * 3 // 18)
    second = (own - first) // 2
    return [size for size in (first, second, own - first - second) if size]


def per_device(buoy, vel_w, strat, eig_val, eig_left, eig_right):
    row_count = lax.axis_size("row")
    col_count = lax.axis_size("col")
    blocks = row_count * col_count
    modes_x, modes_y, degree = buoy.shape
    total_x, total_y = modes_x * row_count, modes_y * col_count
    grid_x, grid_y = 3 * total_x // 2, 3 * total_y // 2
    shard = strat.shape[0]
    own = -(-shard // row_count)
    padding = own * row_count - shard
    kernels = modes_y % 128 == 0 and modes_x % 16 == 0 and degree % 128 == 0
    row = lax.axis_index("row")
    col = lax.axis_index("col")


    def by_device(table):
        table = table.reshape(col_count, shard, degree)
        table = np.pad(table, ((0, 0), (0, padding), (0, 0)))
        return table.reshape(blocks, own, degree)

    def exchange(values):
        return lax.all_to_all(values, ("col", "row"), split_axis=0, concat_axis=0, tiled=True)

    levels, slopes, projector = cheb_tables(degree, shard * col_count)
    forward_z = np.stack([by_device(levels.T), by_device(slopes.T)])
    backward_z = by_device(projector)
    along_x = jnp.asarray(np.ascontiguousarray(fourier_eval(total_x, grid_x).T))
    back_x = jnp.asarray(np.ascontiguousarray(fourier_proj(total_x, grid_x).T))
    along_y = jnp.asarray(fourier_eval(total_y, grid_y))
    back_y = jnp.asarray(np.ascontiguousarray(fourier_proj(total_y, grid_y)))
    strat_own = lax.dynamic_slice_in_dim(jnp.pad(strat, (0, padding)), row * own, own)

    sizes = chunk_sizes(own)
    stops = np.cumsum(sizes)
    pieces = [(int(stop - size), int(stop)) for size, stop in zip(sizes, stops)]
    arrived = []
    for start, stop in pieces:
        table = forward_z[:, :, start:stop].reshape(2, blocks * (stop - start), degree)
        arrived.append(exchange(lift(kernels, vel_w, buoy, jnp.asarray(table), blocks)))
    order = list(range(1, len(pieces))) + [0]
    folded, after = [], []
    for piece in order:
        start, stop = pieces[piece]
        fluxes = planes(
            kernels,
            arrived[piece],
            strat_own[start:stop],
            along_y,
            along_x,
            back_x,
            back_y,
            col_count,
            after,
        )
        after = [fluxes]
        folded.append(exchange(fluxes))
    projs = [
        backward_z[:, start:stop].reshape(blocks * (stop - start), degree)
        for start, stop in (pieces[piece] for piece in order)
    ]
    if len(pieces) > 1:
        table = jnp.asarray(np.concatenate(projs[:-1], axis=0))
        modal = gather(kernels, folded[:-1], table, eig_left, [buoy, vel_w])
    else:
        modal = [
            jnp.einsum("akn,nj->akj", part, eig_left, preferred_element_type=F32)
            for part in (buoy, vel_w)
        ]
    last = jnp.dot(jnp.asarray(projs[-1]), eig_left, preferred_element_type=F32)
    last = (explicit_step * last).astype(BF16)
    wave_x = wave_squares(total_x, row * modes_x, modes_x)
    wave_y = wave_squares(total_y, col * modes_y, modes_y)
    return finish(kernels, folded[-1], last, modal, eig_val, eig_right, wave_x, wave_y)


def solution(mesh):
    in_specs = (P("row", "col", None), P("row", "col", None), P("col"), P(), P(), P())
    out_specs = (P("row", "col", None), P("row", "col", None))
    return jax.shard_map(
        per_device, mesh=mesh, in_specs=in_specs, out_specs=out_specs, check_vma=False
    )
```

```python
import math

import jax
import jax.numpy as jnp
import numpy as np
from jax import lax
from jax.experimental import pallas as pl
from jax.experimental.pallas import tpu as pltpu
from jax.sharding import PartitionSpec as P

explicit_step = 0.5
diffuse_buoy = 0.5
diffuse_vel = 0.25
couple_buoy = 0.7
couple_vel = 0.7

BF16 = jnp.bfloat16
F32 = jnp.float32
VMEM_BYTES = 56 * 1024 * 1024


def fourier_trig(modes, points):
    order = np.arange(modes, dtype=np.int32)
    freq = ((order + 1) // 2).astype(np.float32)
    place = np.arange(points, dtype=np.float32)
    angle = np.float32(2.0 * math.pi / points) * freq[:, None] * place[None, :]
    return (order, np.where((order % 2 == 0)[:, None], np.cos(angle), np.sin(angle)))


def fourier_eval(modes, points):
    order, values = fourier_trig(modes, points)
    return (values * np.float32(math.sqrt(2.0 / modes))).astype(BF16)


def fourier_proj(modes, points):
    order, values = fourier_trig(modes, points)
    weight = np.where(order == 0, 1.0 / points, 2.0 / points).astype(np.float32)
    return np.transpose(values * weight[:, None] * np.float32(math.sqrt(modes / 2.0))).astype(BF16)


def cheb_tables(degree, points):
    order = np.arange(degree, dtype=np.float32)
    theta = np.float32(math.pi) * (np.arange(points, dtype=np.float32) + np.float32(0.5)) / np.float32(points)
    angle = order[:, None] * theta[None, :]
    norm = np.float32(math.sqrt(2.0 / degree))
    levels = np.cos(angle) * norm
    slopes = -(order[:, None] / np.float32(degree)) * np.sin(angle) * norm
    weight = np.where(order == 0, 1.0 / points, 2.0 / points).astype(np.float32)
    projector = np.transpose(np.cos(angle) * weight[:, None] * np.float32(math.sqrt(degree / 2.0)))
    return (levels.astype(BF16), slopes.astype(BF16), projector.astype(BF16))


def wave_squares(modes, offset, count):
    order = offset + jnp.arange(count, dtype=jnp.int32)
    freq = ((order + 1) // 2).astype(F32) * (2.0 / modes)
    return freq * freq


def params(grid_rank):
    return pltpu.CompilerParams(
        dimension_semantics=("arbitrary",) * grid_rank, vmem_limit_bytes=VMEM_BYTES
    )


def whole(shape):
    return pl.BlockSpec(shape, lambda *_: (0,) * len(shape))


def lift_kernel(vel_ref, buoy_ref, table_ref, out_ref):
    blocks, fields, depth, span, lanes = out_ref.shape
    for field, source in enumerate((vel_ref, buoy_ref)):
        coeffs = source[...].reshape(span * lanes, source.shape[-1])
        values = lax.dot_general(
            table_ref[field], coeffs, (((1,), (1,)), ((), ())), preferred_element_type=F32
        )
        values = values.reshape(blocks * depth, span, lanes).astype(BF16)
        out_ref[:, field] = values.reshape(blocks, depth, span, lanes)


def lift(kernels, vel_w, buoy, table, blocks):
    modes_x, modes_y, degree = vel_w.shape
    depth = table.shape[1] // blocks
    shape = (blocks, 2, depth, modes_x, modes_y)
    if not kernels:
        fields = jnp.stack([vel_w, buoy])
        values = jnp.einsum("fzn,fakn->fzak", table, fields, preferred_element_type=F32)
        values = values.astype(BF16).reshape(2, blocks, depth, modes_x, modes_y)
        return jnp.transpose(values, (1, 0, 2, 3, 4))
    span = 16
    return pl.pallas_call(
        lift_kernel,
        grid=(modes_x // span,),
        in_specs=[
            pl.BlockSpec((span, modes_y, degree), lambda a: (a, 0, 0)),
            pl.BlockSpec((span, modes_y, degree), lambda a: (a, 0, 0)),
            whole(table.shape),
        ],
        out_specs=pl.BlockSpec((blocks, 2, depth, span, modes_y), lambda a: (0, 0, 0, a, 0)),
        out_shape=jax.ShapeDtypeStruct(shape, BF16),
        compiler_params=params(1),
        cost_estimate=pl.CostEstimate(
            flops=2 * math.prod(shape) * degree,
            bytes_accessed=2 * (2 * vel_w.size + math.prod(shape)),
            transcendentals=0,
        ),
        name="lift",
    )(vel_w, buoy, table)


def plane_kernel(
    col_count, count, strat_ref, along_y_ref, along_x_ref, back_x_ref, back_y_ref, in_ref, *refs
):
    out_refs = refs[-count:]
    blocks, _, depth, modes_x, lanes = in_ref.shape
    row_count = blocks // col_count
    for level in range(depth):
        grids = []
        for field in range(2):
            rows = []
            for row in range(row_count):
                parts = [in_ref[col * row_count + row, field, level] for col in range(col_count)]
                rows.append(jnp.concatenate(parts, axis=1))
            middle = jnp.dot(
                jnp.concatenate(rows, axis=0), along_y_ref[...], preferred_element_type=F32
            ).astype(BF16)
            grid = jnp.dot(along_x_ref[...], middle, preferred_element_type=F32)
            grids.append(grid.astype(BF16).astype(F32))
        velocity, gradient = grids
        strata = strat_ref[pl.program_id(0) * depth + level]
        flux_buoy = (-(velocity * gradient) - strata * velocity).astype(BF16)
        flux_vel = (-(velocity * jnp.abs(velocity))).astype(BF16)
        for field, flux in enumerate((flux_buoy, flux_vel)):
            folded = jnp.dot(back_x_ref[...], flux, preferred_element_type=F32).astype(BF16)
            values = jnp.dot(folded, back_y_ref[...], preferred_element_type=F32).astype(BF16)
            for row in range(row_count):
                first = row * modes_x
                for out_ref in out_refs:
                    last = first + out_ref.shape[3]
                    for col in range(col_count):
                        out_ref[col * row_count + row, field, level] = values[
                            first:last, col * lanes : (col + 1) * lanes
                        ]
                    first = last


def planes(kernels, arrived, strat, along_y, along_x, back_x, back_y, col_count, splits, after):
    blocks, fields, depth, modes_x, modes_y = arrived.shape
    row_count = blocks // col_count
    if not kernels:
        parts = arrived.reshape(col_count, row_count, fields, depth, modes_x, modes_y)
        parts = jnp.transpose(parts, (2, 3, 1, 4, 0, 5))
        parts = parts.reshape(fields, depth, row_count * modes_x, col_count * modes_y)
        middle = jnp.einsum("fzak,ky->fzay", parts, along_y, preferred_element_type=F32)
        grids = jnp.einsum("xa,fzay->fzxy", along_x, middle.astype(BF16), preferred_element_type=F32)
        grids = grids.astype(BF16).astype(F32)
        flux_buoy = -(grids[0] * grids[1]) - strat[:, None, None] * grids[0]
        flux_vel = -(grids[0] * jnp.abs(grids[0]))
        fluxes = jnp.stack([flux_buoy, flux_vel]).astype(BF16)
        folded = jnp.einsum("ax,fzxy->fzay", back_x, fluxes, preferred_element_type=F32)
        values = jnp.einsum("fzay,yk->fzak", folded.astype(BF16), back_y, preferred_element_type=F32)
        values = values.astype(BF16).reshape(
            fields, depth, row_count, modes_x, col_count, modes_y
        )
        values = jnp.transpose(values, (4, 2, 0, 1, 3, 5)).reshape(arrived.shape)
        return jnp.split(values, np.cumsum(splits)[:-1], axis=3)
    block = pl.BlockSpec((blocks, fields, 1, modes_x, modes_y), lambda z: (0, 0, z, 0, 0))
    work = along_y.size * along_x.shape[1] + along_x.size * along_y.shape[1]
    return pl.pallas_call(
        lambda *refs: plane_kernel(col_count, len(splits), *refs),
        grid=(depth,),
        in_specs=[
            pl.BlockSpec(memory_space=pltpu.SMEM),
            whole(along_y.shape),
            whole(along_x.shape),
            whole(back_x.shape),
            whole(back_y.shape),
            block,
        ]
        + [pl.BlockSpec(memory_space=pl.ANY)] * len(after),
        out_specs=[
            pl.BlockSpec((blocks, fields, 1, size, modes_y), lambda z: (0, 0, z, 0, 0))
            for size in splits
        ],
        out_shape=[
            jax.ShapeDtypeStruct((blocks, fields, depth, size, modes_y), BF16) for size in splits
        ],
        compiler_params=params(1),
        cost_estimate=pl.CostEstimate(
            flops=4 * fields * depth * work, bytes_accessed=4 * arrived.size, transcendentals=0
        ),
        name="planes",
    )(strat, along_y, along_x, back_x, back_y, arrived, *after)


def solve_modal(modal_buoy, modal_vel, wave, eig_val):
    diag_buoy = (1.0 + diffuse_buoy * wave) + diffuse_buoy * eig_val
    diag_vel = (1.0 + diffuse_vel * wave) + diffuse_vel * eig_val
    scale = 1.0 / (diag_buoy * diag_vel + couple_buoy * couple_vel)
    modal_buoy = modal_buoy * scale
    modal_vel = modal_vel * scale
    solved_buoy = (diag_vel * modal_buoy - couple_buoy * modal_vel).astype(BF16)
    solved_vel = (diag_buoy * modal_vel + couple_vel * modal_buoy).astype(BF16)
    return (solved_buoy, solved_vel)


def project(refs, field, proj_ref):
    blocks, _, _, span, lanes = refs[0].shape
    parts = [ref[:, field].reshape(blocks * ref.shape[2], span, lanes) for ref in refs]
    fluxes = jnp.concatenate(parts, axis=0).astype(F32)
    fluxes = jnp.swapaxes(fluxes, 0, 1).astype(BF16)
    rows = [jnp.transpose(fluxes[mode]) for mode in range(span)]
    return jnp.dot(jnp.concatenate(rows, axis=0), proj_ref[...], preferred_element_type=F32)


def finish_kernel(
    count,
    wave_x_ref,
    wave_y_ref,
    eig_val_ref,
    left_ref,
    right_ref,
    proj_ref,
    buoy_ref,
    vel_ref,
    *refs,
):
    in_refs, out_refs = refs[:count], refs[-2:]
    span, lanes, degree = buoy_ref.shape
    modal = []
    for field, coeff_ref in enumerate((buoy_ref, vel_ref)):
        tend = explicit_step * project(in_refs, field, proj_ref)
        rhs = coeff_ref[...].reshape(span * lanes, degree).astype(F32) + tend
        modal.append(jnp.dot(rhs.astype(BF16), left_ref[...], preferred_element_type=F32))
    first = pl.program_id(0) * span
    waves = [4.0 * (wave_x_ref[first + mode] + wave_y_ref[...]) for mode in range(span)]
    solved = solve_modal(modal[0], modal[1], jnp.concatenate(waves, axis=0), eig_val_ref[...])
    for values, out_ref in zip(solved, out_refs):
        result = jnp.dot(values, right_ref[...], preferred_element_type=F32).astype(BF16)
        out_ref[...] = result.reshape(span, lanes, degree)


def finish(
    kernels, start, size, parts, proj, buoy, vel_w, eigen, wave_x, wave_y, earlier
):
    eig_val, eig_left, eig_right = eigen
    modes_y, degree = buoy.shape[1:]
    wave_x = wave_x[start : start + size]
    if not kernels:
        taken = [part[:, :, :, start - first :][:, :, :, :size] for first, part in parts]
        taken = [
            jnp.transpose(part, (1, 0, 2, 3, 4)).reshape(2, -1, size, modes_y) for part in taken
        ]
        tend = jnp.einsum(
            "fzak,zn->fakn", jnp.concatenate(taken, axis=1), proj, preferred_element_type=F32
        )
        fields = jnp.stack([buoy, vel_w])[:, start : start + size].astype(F32)
        rhs = (fields + explicit_step * tend).astype(BF16)
        modal = jnp.einsum("fakn,nj->fakj", rhs, eig_left, preferred_element_type=F32)
        wave = 4.0 * (wave_x[:, None, None] + wave_y[None, :, None])
        results = [
            jnp.einsum("akj,jn->akn", values, eig_right, preferred_element_type=F32).astype(BF16)
            for values in solve_modal(modal[0], modal[1], wave, eig_val)
        ]
        if earlier:
            results = [jnp.concatenate(pair, axis=0) for pair in zip(earlier, results)]
        return results
    span = 8
    block = pl.BlockSpec((span, modes_y, degree), lambda a: (a + start // span, 0, 0))

    def part_spec(first, part):
        return pl.BlockSpec(
            (*part.shape[:3], span, modes_y), lambda a: (0, 0, 0, a + (start - first) // span, 0)
        )

    result = jax.ShapeDtypeStruct(buoy.shape, BF16)
    operands = [wave_x, wave_y[:, None], eig_val[None, :], eig_left, eig_right, proj, buoy, vel_w]
    operands += [part for _, part in parts]
    return pl.pallas_call(
        lambda *refs: finish_kernel(len(parts), *refs),
        grid=(size // span,),
        in_specs=[
            pl.BlockSpec(memory_space=pltpu.SMEM),
            whole((modes_y, 1)),
            whole((1, degree)),
            whole(eig_left.shape),
            whole(eig_right.shape),
            whole(proj.shape),
            block,
            block,
        ]
        + [part_spec(first, part) for first, part in parts]
        + [pl.BlockSpec(memory_space=pl.ANY)] * len(earlier),
        out_specs=[block, block],
        out_shape=[result, result],
        input_output_aliases={len(operands) + item: item for item in range(len(earlier))},
        compiler_params=params(1),
        cost_estimate=pl.CostEstimate(
            flops=4 * size * modes_y * degree * (proj.shape[0] + 2 * degree),
            bytes_accessed=size * modes_y * (8 * degree + 4 * proj.shape[0]),
            transcendentals=size * modes_y * degree,
        ),
        name="finish",
    )(*operands, *earlier)


def chunk_sizes(own):
    first = -(-own * 4 // 18)
    return [size for size in (first, own - first) if size]


def per_device(buoy, vel_w, strat, eig_val, eig_left, eig_right):
    row_count = lax.axis_size("row")
    col_count = lax.axis_size("col")
    blocks = row_count * col_count
    modes_x, modes_y, degree = buoy.shape
    total_x, total_y = modes_x * row_count, modes_y * col_count
    grid_x, grid_y = 3 * total_x // 2, 3 * total_y // 2
    shard = strat.shape[0]
    own = -(-shard // row_count)
    padding = own * row_count - shard
    kernels = modes_y % 128 == 0 and modes_x % 64 == 0 and degree % 128 == 0
    row = lax.axis_index("row")
    col = lax.axis_index("col")


    def by_device(table):
        table = table.reshape(col_count, shard, degree)
        table = np.pad(table, ((0, 0), (0, padding), (0, 0)))
        return table.reshape(blocks, own, degree)

    def exchange(values):
        return lax.all_to_all(values, ("col", "row"), split_axis=0, concat_axis=0, tiled=True)

    levels, slopes, projector = cheb_tables(degree, shard * col_count)
    forward_z = np.stack([by_device(levels.T), by_device(slopes.T)])
    backward_z = by_device(projector)
    along_x = jnp.asarray(np.ascontiguousarray(fourier_eval(total_x, grid_x).T))
    back_x = jnp.asarray(np.ascontiguousarray(fourier_proj(total_x, grid_x).T))
    along_y = jnp.asarray(fourier_eval(total_y, grid_y))
    back_y = jnp.asarray(np.ascontiguousarray(fourier_proj(total_y, grid_y)))
    strat_own = lax.dynamic_slice_in_dim(jnp.pad(strat, (0, padding)), row * own, own)

    sizes = chunk_sizes(own)
    stops = np.cumsum(sizes)
    pieces = [(int(stop - size), int(stop)) for size, stop in zip(sizes, stops)]
    arrived = []
    for start, stop in pieces:
        table = forward_z[:, :, start:stop].reshape(2, blocks * (stop - start), degree)
        arrived.append(exchange(lift(kernels, vel_w, buoy, jnp.asarray(table), blocks)))
    split = modes_x - modes_x // 4
    parts, after = [], []
    for values, (start, stop) in zip(arrived, pieces):
        splits = [split, modes_x - split] if stop == own else [modes_x]
        after = planes(
            kernels,
            values,
            strat_own[start:stop],
            along_y,
            along_x,
            back_x,
            back_y,
            col_count,
            splits,
            after,
        )
        parts.append([exchange(fluxes) for fluxes in after])
    proj = [
        backward_z[:, start:stop].reshape(blocks * (stop - start), degree)
        for start, stop in pieces
    ]
    proj = jnp.asarray(np.concatenate(proj, axis=0))
    wave_x = wave_squares(total_x, row * modes_x, modes_x)
    wave_y = wave_squares(total_y, col * modes_y, modes_y)
    eigen = (eig_val, eig_left, eig_right)
    results = []
    for start, size, fluxes in ((0, split, parts[-1][0]), (split, modes_x - split, parts[-1][1])):
        held = [(0, part[0]) for part in parts[:-1]] + [(start, fluxes)]
        results = finish(
            kernels, start, size, held, proj, buoy, vel_w, eigen, wave_x, wave_y, results
        )
    return tuple(results)


def solution(mesh):
    in_specs = (P("row", "col", None), P("row", "col", None), P("col"), P(), P(), P())
    out_specs = (P("row", "col", None), P("row", "col", None))
    return jax.shard_map(
        per_device, mesh=mesh, in_specs=in_specs, out_specs=out_specs, check_vma=False
    )
```

```python
import math

import jax
import jax.numpy as jnp
import numpy as np
from jax import lax
from jax.experimental import pallas as pl
from jax.experimental.pallas import tpu as pltpu
from jax.sharding import PartitionSpec as P

explicit_step = 0.5
diffuse_buoy = 0.5
diffuse_vel = 0.25
couple_buoy = 0.7
couple_vel = 0.7

BF16 = jnp.bfloat16
F32 = jnp.float32
VMEM_BYTES = 63 * 1024 * 1024


def fourier_trig(modes, points):
    order = np.arange(modes, dtype=np.int32)
    freq = ((order + 1) // 2).astype(np.float32)
    place = np.arange(points, dtype=np.float32)
    angle = np.float32(2.0 * math.pi / points) * freq[:, None] * place[None, :]
    return (order, np.where((order % 2 == 0)[:, None], np.cos(angle), np.sin(angle)))


def fourier_eval(modes, points):
    order, values = fourier_trig(modes, points)
    return (values * np.float32(math.sqrt(2.0 / modes))).astype(BF16)


def fourier_proj(modes, points):
    order, values = fourier_trig(modes, points)
    weight = np.where(order == 0, 1.0 / points, 2.0 / points).astype(np.float32)
    return np.transpose(values * weight[:, None] * np.float32(math.sqrt(modes / 2.0))).astype(BF16)


def cheb_tables(degree, points):
    order = np.arange(degree, dtype=np.float32)
    theta = np.float32(math.pi) * (np.arange(points, dtype=np.float32) + np.float32(0.5)) / np.float32(points)
    angle = order[:, None] * theta[None, :]
    norm = np.float32(math.sqrt(2.0 / degree))
    levels = np.cos(angle) * norm
    slopes = -(order[:, None] / np.float32(degree)) * np.sin(angle) * norm
    weight = np.where(order == 0, 1.0 / points, 2.0 / points).astype(np.float32)
    projector = np.transpose(np.cos(angle) * weight[:, None] * np.float32(math.sqrt(degree / 2.0)))
    return (levels.astype(BF16), slopes.astype(BF16), projector.astype(BF16))


def wave_squares(modes, offset, count):
    order = offset + jnp.arange(count, dtype=jnp.int32)
    freq = ((order + 1) // 2).astype(F32) * (2.0 / modes)
    return freq * freq


def params(grid_rank):
    return pltpu.CompilerParams(
        dimension_semantics=("arbitrary",) * grid_rank, vmem_limit_bytes=VMEM_BYTES
    )


def whole(shape):
    return pl.BlockSpec(shape, lambda *_: (0,) * len(shape))


def lift_kernel(vel_ref, buoy_ref, table_ref, out_ref):
    blocks, fields, depth, span, lanes = out_ref.shape
    for field, source in enumerate((vel_ref, buoy_ref)):
        coeffs = source[...].reshape(span * lanes, source.shape[-1])
        values = lax.dot_general(
            table_ref[field], coeffs, (((1,), (1,)), ((), ())), preferred_element_type=F32
        )
        values = values.reshape(blocks * depth, span, lanes).astype(BF16)
        out_ref[:, field] = values.reshape(blocks, depth, span, lanes)


def lift(kernels, vel_w, buoy, table, blocks):
    modes_x, modes_y, degree = vel_w.shape
    depth = table.shape[1] // blocks
    shape = (blocks, 2, depth, modes_x, modes_y)
    if not kernels:
        fields = jnp.stack([vel_w, buoy])
        values = jnp.einsum("fzn,fakn->fzak", table, fields, preferred_element_type=F32)
        values = values.astype(BF16).reshape(2, blocks, depth, modes_x, modes_y)
        return jnp.transpose(values, (1, 0, 2, 3, 4))
    span = 16
    return pl.pallas_call(
        lift_kernel,
        grid=(modes_x // span,),
        in_specs=[
            pl.BlockSpec((span, modes_y, degree), lambda a: (a, 0, 0)),
            pl.BlockSpec((span, modes_y, degree), lambda a: (a, 0, 0)),
            whole(table.shape),
        ],
        out_specs=pl.BlockSpec((blocks, 2, depth, span, modes_y), lambda a: (0, 0, 0, a, 0)),
        out_shape=jax.ShapeDtypeStruct(shape, BF16),
        compiler_params=params(1),
        cost_estimate=pl.CostEstimate(
            flops=2 * math.prod(shape) * degree,
            bytes_accessed=2 * (2 * vel_w.size + math.prod(shape)),
            transcendentals=0,
        ),
        name="lift",
    )(vel_w, buoy, table)


def plane_kernel(
    col_count, count, strat_ref, along_y_ref, along_x_ref, back_x_ref, back_y_ref, in_ref, *refs
):
    out_refs = refs[-count:]
    blocks, _, depth, modes_x, lanes = in_ref.shape
    row_count = blocks // col_count
    for level in range(depth):
        grids = []
        for field in range(2):
            rows = []
            for row in range(row_count):
                parts = [in_ref[col * row_count + row, field, level] for col in range(col_count)]
                rows.append(jnp.concatenate(parts, axis=1))
            middle = jnp.dot(
                jnp.concatenate(rows, axis=0), along_y_ref[...], preferred_element_type=F32
            ).astype(BF16)
            grid = jnp.dot(along_x_ref[...], middle, preferred_element_type=F32)
            grids.append(grid.astype(BF16).astype(F32))
        velocity, gradient = grids
        strata = strat_ref[pl.program_id(0) * depth + level]
        flux_buoy = (-(velocity * gradient) - strata * velocity).astype(BF16)
        flux_vel = (-(velocity * jnp.abs(velocity))).astype(BF16)
        for field, flux in enumerate((flux_buoy, flux_vel)):
            folded = jnp.dot(back_x_ref[...], flux, preferred_element_type=F32).astype(BF16)
            values = jnp.dot(folded, back_y_ref[...], preferred_element_type=F32).astype(BF16)
            for row in range(row_count):
                first = row * modes_x
                for out_ref in out_refs:
                    last = first + out_ref.shape[3]
                    for col in range(col_count):
                        out_ref[col * row_count + row, field, level] = values[
                            first:last, col * lanes : (col + 1) * lanes
                        ]
                    first = last


def planes(kernels, arrived, strat, along_y, along_x, back_x, back_y, col_count, splits, after):
    blocks, fields, depth, modes_x, modes_y = arrived.shape
    row_count = blocks // col_count
    if not kernels:
        parts = arrived.reshape(col_count, row_count, fields, depth, modes_x, modes_y)
        parts = jnp.transpose(parts, (2, 3, 1, 4, 0, 5))
        parts = parts.reshape(fields, depth, row_count * modes_x, col_count * modes_y)
        middle = jnp.einsum("fzak,ky->fzay", parts, along_y, preferred_element_type=F32)
        grids = jnp.einsum("xa,fzay->fzxy", along_x, middle.astype(BF16), preferred_element_type=F32)
        grids = grids.astype(BF16).astype(F32)
        flux_buoy = -(grids[0] * grids[1]) - strat[:, None, None] * grids[0]
        flux_vel = -(grids[0] * jnp.abs(grids[0]))
        fluxes = jnp.stack([flux_buoy, flux_vel]).astype(BF16)
        folded = jnp.einsum("ax,fzxy->fzay", back_x, fluxes, preferred_element_type=F32)
        values = jnp.einsum("fzay,yk->fzak", folded.astype(BF16), back_y, preferred_element_type=F32)
        values = values.astype(BF16).reshape(
            fields, depth, row_count, modes_x, col_count, modes_y
        )
        values = jnp.transpose(values, (4, 2, 0, 1, 3, 5)).reshape(arrived.shape)
        return jnp.split(values, np.cumsum(splits)[:-1], axis=3)
    block = pl.BlockSpec((blocks, fields, 1, modes_x, modes_y), lambda z: (0, 0, z, 0, 0))
    work = along_y.size * along_x.shape[1] + along_x.size * along_y.shape[1]
    return pl.pallas_call(
        lambda *refs: plane_kernel(col_count, len(splits), *refs),
        grid=(depth,),
        in_specs=[
            pl.BlockSpec(memory_space=pltpu.SMEM),
            whole(along_y.shape),
            whole(along_x.shape),
            whole(back_x.shape),
            whole(back_y.shape),
            block,
        ]
        + [pl.BlockSpec(memory_space=pl.ANY)] * len(after),
        out_specs=[
            pl.BlockSpec((blocks, fields, 1, size, modes_y), lambda z: (0, 0, z, 0, 0))
            for size in splits
        ],
        out_shape=[
            jax.ShapeDtypeStruct((blocks, fields, depth, size, modes_y), BF16) for size in splits
        ],
        compiler_params=params(1),
        cost_estimate=pl.CostEstimate(
            flops=4 * fields * depth * work, bytes_accessed=4 * arrived.size, transcendentals=0
        ),
        name="planes",
    )(strat, along_y, along_x, back_x, back_y, arrived, *after)


def solve_modal(modal_buoy, modal_vel, wave, eig_val):
    diag_buoy = (1.0 + diffuse_buoy * wave) + diffuse_buoy * eig_val
    diag_vel = (1.0 + diffuse_vel * wave) + diffuse_vel * eig_val
    scale = 1.0 / (diag_buoy * diag_vel + couple_buoy * couple_vel)
    modal_buoy = modal_buoy * scale
    modal_vel = modal_vel * scale
    solved_buoy = (diag_vel * modal_buoy - couple_buoy * modal_vel).astype(BF16)
    solved_vel = (diag_buoy * modal_vel + couple_vel * modal_buoy).astype(BF16)
    return (solved_buoy, solved_vel)


def project(refs, field, proj_ref):
    blocks, _, _, span, lanes = refs[0].shape
    parts = [ref[:, field].reshape(blocks * ref.shape[2], span, lanes) for ref in refs]
    fluxes = jnp.concatenate(parts, axis=0).astype(F32)
    fluxes = jnp.swapaxes(fluxes, 0, 1).astype(BF16)
    rows = [jnp.transpose(fluxes[mode]) for mode in range(span)]
    return jnp.dot(jnp.concatenate(rows, axis=0), proj_ref[...], preferred_element_type=F32)


def finish_kernel(
    count,
    wave_x_ref,
    wave_y_ref,
    eig_val_ref,
    left_ref,
    right_ref,
    proj_ref,
    buoy_ref,
    vel_ref,
    *refs,
):
    in_refs, out_refs = refs[:count], refs[-2:]
    span, lanes, degree = buoy_ref.shape
    modal = []
    for field, coeff_ref in enumerate((buoy_ref, vel_ref)):
        tend = explicit_step * project(in_refs, field, proj_ref)
        rhs = coeff_ref[...].reshape(span * lanes, degree).astype(F32) + tend
        modal.append(jnp.dot(rhs.astype(BF16), left_ref[...], preferred_element_type=F32))
    first = pl.program_id(0) * span
    waves = [4.0 * (wave_x_ref[first + mode] + wave_y_ref[...]) for mode in range(span)]
    solved = solve_modal(modal[0], modal[1], jnp.concatenate(waves, axis=0), eig_val_ref[...])
    for values, out_ref in zip(solved, out_refs):
        result = jnp.dot(values, right_ref[...], preferred_element_type=F32).astype(BF16)
        out_ref[...] = result.reshape(span, lanes, degree)


def finish(
    kernels, start, size, parts, proj, buoy, vel_w, eigen, wave_x, wave_y, earlier
):
    eig_val, eig_left, eig_right = eigen
    modes_y, degree = buoy.shape[1:]
    wave_x = wave_x[start : start + size]
    if not kernels:
        taken = [part[:, :, :, start - first :][:, :, :, :size] for first, part in parts]
        taken = [
            jnp.transpose(part, (1, 0, 2, 3, 4)).reshape(2, -1, size, modes_y) for part in taken
        ]
        tend = jnp.einsum(
            "fzak,zn->fakn", jnp.concatenate(taken, axis=1), proj, preferred_element_type=F32
        )
        fields = jnp.stack([buoy, vel_w])[:, start : start + size].astype(F32)
        rhs = (fields + explicit_step * tend).astype(BF16)
        modal = jnp.einsum("fakn,nj->fakj", rhs, eig_left, preferred_element_type=F32)
        wave = 4.0 * (wave_x[:, None, None] + wave_y[None, :, None])
        results = [
            jnp.einsum("akj,jn->akn", values, eig_right, preferred_element_type=F32).astype(BF16)
            for values in solve_modal(modal[0], modal[1], wave, eig_val)
        ]
        if earlier:
            results = [jnp.concatenate(pair, axis=0) for pair in zip(earlier, results)]
        return results
    span = 8
    block = pl.BlockSpec((span, modes_y, degree), lambda a: (a + start // span, 0, 0))

    def part_spec(first, part):
        return pl.BlockSpec(
            (*part.shape[:3], span, modes_y), lambda a: (0, 0, 0, a + (start - first) // span, 0)
        )

    result = jax.ShapeDtypeStruct(buoy.shape, BF16)
    operands = [wave_x, wave_y[:, None], eig_val[None, :], eig_left, eig_right, proj, buoy, vel_w]
    operands += [part for _, part in parts]
    return pl.pallas_call(
        lambda *refs: finish_kernel(len(parts), *refs),
        grid=(size // span,),
        in_specs=[
            pl.BlockSpec(memory_space=pltpu.SMEM),
            whole((modes_y, 1)),
            whole((1, degree)),
            whole(eig_left.shape),
            whole(eig_right.shape),
            whole(proj.shape),
            block,
            block,
        ]
        + [part_spec(first, part) for first, part in parts]
        + [pl.BlockSpec(memory_space=pl.ANY)] * len(earlier),
        out_specs=[block, block],
        out_shape=[result, result],
        input_output_aliases={len(operands) + item: item for item in range(len(earlier))},
        compiler_params=params(1),
        cost_estimate=pl.CostEstimate(
            flops=4 * size * modes_y * degree * (proj.shape[0] + 2 * degree),
            bytes_accessed=size * modes_y * (8 * degree + 4 * proj.shape[0]),
            transcendentals=size * modes_y * degree,
        ),
        name="finish",
    )(*operands, *earlier)


def chunk_sizes(own):
    first = -(-own * 4 // 18)
    return [size for size in (first, own - first) if size]


def per_device(buoy, vel_w, strat, eig_val, eig_left, eig_right):
    row_count = lax.axis_size("row")
    col_count = lax.axis_size("col")
    blocks = row_count * col_count
    modes_x, modes_y, degree = buoy.shape
    total_x, total_y = modes_x * row_count, modes_y * col_count
    grid_x, grid_y = 3 * total_x // 2, 3 * total_y // 2
    shard = strat.shape[0]
    own = -(-shard // row_count)
    padding = own * row_count - shard
    kernels = modes_y % 128 == 0 and modes_x % 64 == 0 and degree % 128 == 0
    row = lax.axis_index("row")
    col = lax.axis_index("col")


    def by_device(table):
        table = table.reshape(col_count, shard, degree)
        table = np.pad(table, ((0, 0), (0, padding), (0, 0)))
        return table.reshape(blocks, own, degree)

    def exchange(values):
        return lax.all_to_all(values, ("col", "row"), split_axis=0, concat_axis=0, tiled=True)

    levels, slopes, projector = cheb_tables(degree, shard * col_count)
    forward_z = np.stack([by_device(levels.T), by_device(slopes.T)])
    backward_z = by_device(projector)
    along_x = jnp.asarray(np.ascontiguousarray(fourier_eval(total_x, grid_x).T))
    back_x = jnp.asarray(np.ascontiguousarray(fourier_proj(total_x, grid_x).T))
    along_y = jnp.asarray(fourier_eval(total_y, grid_y))
    back_y = jnp.asarray(np.ascontiguousarray(fourier_proj(total_y, grid_y)))
    strat_own = lax.dynamic_slice_in_dim(jnp.pad(strat, (0, padding)), row * own, own)

    sizes = chunk_sizes(own)
    stops = np.cumsum(sizes)
    pieces = [(int(stop - size), int(stop)) for size, stop in zip(sizes, stops)]
    arrived = []
    for start, stop in pieces:
        table = forward_z[:, :, start:stop].reshape(2, blocks * (stop - start), degree)
        arrived.append(exchange(lift(kernels, vel_w, buoy, jnp.asarray(table), blocks)))
    split = modes_x - modes_x // 8
    parts, after = [], []
    for values, (start, stop) in zip(arrived, pieces):
        splits = [split, modes_x - split] if stop == own else [modes_x]
        after = planes(
            kernels,
            values,
            strat_own[start:stop],
            along_y,
            along_x,
            back_x,
            back_y,
            col_count,
            splits,
            after,
        )
        parts.append([exchange(fluxes) for fluxes in after])
    proj = [
        backward_z[:, start:stop].reshape(blocks * (stop - start), degree)
        for start, stop in pieces
    ]
    proj = jnp.asarray(np.concatenate(proj, axis=0))
    wave_x = wave_squares(total_x, row * modes_x, modes_x)
    wave_y = wave_squares(total_y, col * modes_y, modes_y)
    eigen = (eig_val, eig_left, eig_right)
    results = []
    for start, size, fluxes in ((0, split, parts[-1][0]), (split, modes_x - split, parts[-1][1])):
        held = [(0, part[0]) for part in parts[:-1]] + [(start, fluxes)]
        results = finish(
            kernels, start, size, held, proj, buoy, vel_w, eigen, wave_x, wave_y, results
        )
    return tuple(results)


def solution(mesh):
    in_specs = (P("row", "col", None), P("row", "col", None), P("col"), P(), P(), P())
    out_specs = (P("row", "col", None), P("row", "col", None))
    return jax.shard_map(
        per_device, mesh=mesh, in_specs=in_specs, out_specs=out_specs, check_vma=False
    )
```

```python
import math

import jax
import jax.numpy as jnp
import numpy as np
from jax import lax
from jax.experimental import pallas as pl
from jax.experimental.pallas import tpu as pltpu
from jax.sharding import PartitionSpec as P

explicit_step = 0.5
diffuse_buoy = 0.5
diffuse_vel = 0.25
couple_buoy = 0.7
couple_vel = 0.7

BF16 = jnp.bfloat16
F32 = jnp.float32
VMEM_BYTES = 63 * 1024 * 1024


def fourier_trig(modes, points):
    order = np.arange(modes, dtype=np.int32)
    freq = ((order + 1) // 2).astype(np.float32)
    place = np.arange(points, dtype=np.float32)
    angle = np.float32(2.0 * math.pi / points) * freq[:, None] * place[None, :]
    return (order, np.where((order % 2 == 0)[:, None], np.cos(angle), np.sin(angle)))


def fourier_eval(modes, points):
    order, values = fourier_trig(modes, points)
    return (values * np.float32(math.sqrt(2.0 / modes))).astype(BF16)


def fourier_proj(modes, points):
    order, values = fourier_trig(modes, points)
    weight = np.where(order == 0, 1.0 / points, 2.0 / points).astype(np.float32)
    return np.transpose(values * weight[:, None] * np.float32(math.sqrt(modes / 2.0))).astype(BF16)


def cheb_tables(degree, points):
    order = np.arange(degree, dtype=np.float32)
    theta = np.float32(math.pi) * (np.arange(points, dtype=np.float32) + np.float32(0.5)) / np.float32(points)
    angle = order[:, None] * theta[None, :]
    norm = np.float32(math.sqrt(2.0 / degree))
    levels = np.cos(angle) * norm
    slopes = -(order[:, None] / np.float32(degree)) * np.sin(angle) * norm
    weight = np.where(order == 0, 1.0 / points, 2.0 / points).astype(np.float32)
    projector = np.transpose(np.cos(angle) * weight[:, None] * np.float32(math.sqrt(degree / 2.0)))
    return (levels.astype(BF16), slopes.astype(BF16), projector.astype(BF16))


def wave_squares(modes, offset, count):
    order = offset + jnp.arange(count, dtype=jnp.int32)
    freq = ((order + 1) // 2).astype(F32) * (2.0 / modes)
    return freq * freq


def params(grid_rank):
    return pltpu.CompilerParams(
        dimension_semantics=("arbitrary",) * grid_rank, vmem_limit_bytes=VMEM_BYTES
    )


def whole(shape):
    return pl.BlockSpec(shape, lambda *_: (0,) * len(shape))


def lift_kernel(vel_ref, buoy_ref, table_ref, out_ref):
    blocks, fields, depth, span, lanes = out_ref.shape
    for field, source in enumerate((vel_ref, buoy_ref)):
        coeffs = source[...].reshape(span * lanes, source.shape[-1])
        values = lax.dot_general(
            table_ref[field], coeffs, (((1,), (1,)), ((), ())), preferred_element_type=F32
        )
        values = values.reshape(blocks * depth, span, lanes).astype(BF16)
        out_ref[:, field] = values.reshape(blocks, depth, span, lanes)


def lift(kernels, vel_w, buoy, table, blocks):
    modes_x, modes_y, degree = vel_w.shape
    depth = table.shape[1] // blocks
    shape = (blocks, 2, depth, modes_x, modes_y)
    if not kernels:
        fields = jnp.stack([vel_w, buoy])
        values = jnp.einsum("fzn,fakn->fzak", table, fields, preferred_element_type=F32)
        values = values.astype(BF16).reshape(2, blocks, depth, modes_x, modes_y)
        return jnp.transpose(values, (1, 0, 2, 3, 4))
    span = 16
    return pl.pallas_call(
        lift_kernel,
        grid=(modes_x // span,),
        in_specs=[
            pl.BlockSpec((span, modes_y, degree), lambda a: (a, 0, 0)),
            pl.BlockSpec((span, modes_y, degree), lambda a: (a, 0, 0)),
            whole(table.shape),
        ],
        out_specs=pl.BlockSpec((blocks, 2, depth, span, modes_y), lambda a: (0, 0, 0, a, 0)),
        out_shape=jax.ShapeDtypeStruct(shape, BF16),
        compiler_params=params(1),
        cost_estimate=pl.CostEstimate(
            flops=2 * math.prod(shape) * degree,
            bytes_accessed=2 * (2 * vel_w.size + math.prod(shape)),
            transcendentals=0,
        ),
        name="lift",
    )(vel_w, buoy, table)


def plane_kernel(
    slots, count, strat_ref, along_y_ref, along_x_ref, back_x_ref, back_y_ref, in_ref, *refs
):
    out_refs = refs[-count:]
    _, _, depth, modes_x, lanes = in_ref.shape
    for level in range(depth):
        grids = []
        for field in range(2):
            rows = []
            for cols in slots:
                parts = [in_ref[slot, field, level] for slot in cols]
                rows.append(jnp.concatenate(parts, axis=1))
            middle = jnp.dot(
                jnp.concatenate(rows, axis=0), along_y_ref[...], preferred_element_type=F32
            ).astype(BF16)
            grid = jnp.dot(along_x_ref[...], middle, preferred_element_type=F32)
            grids.append(grid.astype(BF16).astype(F32))
        velocity, gradient = grids
        strata = strat_ref[pl.program_id(0) * depth + level]
        flux_buoy = (-(velocity * gradient) - strata * velocity).astype(BF16)
        flux_vel = (-(velocity * jnp.abs(velocity))).astype(BF16)
        for field, flux in enumerate((flux_buoy, flux_vel)):
            folded = jnp.dot(back_x_ref[...], flux, preferred_element_type=F32).astype(BF16)
            values = jnp.dot(folded, back_y_ref[...], preferred_element_type=F32).astype(BF16)
            for row, cols in enumerate(slots):
                first = row * modes_x
                for out_ref in out_refs:
                    last = first + out_ref.shape[3]
                    for col, slot in enumerate(cols):
                        out_ref[slot, field, level] = values[
                            first:last, col * lanes : (col + 1) * lanes
                        ]
                    first = last


def planes(kernels, arrived, strat, along_y, along_x, back_x, back_y, slots, splits, after):
    blocks, fields, depth, modes_x, modes_y = arrived.shape
    row_count, col_count = len(slots), len(slots[0])
    if not kernels:
        parts = arrived[np.array(slots).reshape(-1)]
        parts = parts.reshape(row_count, col_count, fields, depth, modes_x, modes_y)
        parts = jnp.transpose(parts, (2, 3, 0, 4, 1, 5))
        parts = parts.reshape(fields, depth, row_count * modes_x, col_count * modes_y)
        middle = jnp.einsum("fzak,ky->fzay", parts, along_y, preferred_element_type=F32)
        grids = jnp.einsum("xa,fzay->fzxy", along_x, middle.astype(BF16), preferred_element_type=F32)
        grids = grids.astype(BF16).astype(F32)
        flux_buoy = -(grids[0] * grids[1]) - strat[:, None, None] * grids[0]
        flux_vel = -(grids[0] * jnp.abs(grids[0]))
        fluxes = jnp.stack([flux_buoy, flux_vel]).astype(BF16)
        folded = jnp.einsum("ax,fzxy->fzay", back_x, fluxes, preferred_element_type=F32)
        values = jnp.einsum("fzay,yk->fzak", folded.astype(BF16), back_y, preferred_element_type=F32)
        values = values.astype(BF16).reshape(
            fields, depth, row_count, modes_x, col_count, modes_y
        )
        values = jnp.transpose(values, (2, 4, 0, 1, 3, 5)).reshape(arrived.shape)
        values = values[np.argsort(np.array(slots).reshape(-1))]
        return jnp.split(values, np.cumsum(splits)[:-1], axis=3)
    block = pl.BlockSpec((blocks, fields, 1, modes_x, modes_y), lambda z: (0, 0, z, 0, 0))
    work = along_y.size * along_x.shape[1] + along_x.size * along_y.shape[1]
    return pl.pallas_call(
        lambda *refs: plane_kernel(slots, len(splits), *refs),
        grid=(depth,),
        in_specs=[
            pl.BlockSpec(memory_space=pltpu.SMEM),
            whole(along_y.shape),
            whole(along_x.shape),
            whole(back_x.shape),
            whole(back_y.shape),
            block,
        ]
        + [pl.BlockSpec(memory_space=pl.ANY)] * len(after),
        out_specs=[
            pl.BlockSpec((blocks, fields, 1, size, modes_y), lambda z: (0, 0, z, 0, 0))
            for size in splits
        ],
        out_shape=[
            jax.ShapeDtypeStruct((blocks, fields, depth, size, modes_y), BF16) for size in splits
        ],
        compiler_params=params(1),
        cost_estimate=pl.CostEstimate(
            flops=4 * fields * depth * work, bytes_accessed=4 * arrived.size, transcendentals=0
        ),
        name="planes",
    )(strat, along_y, along_x, back_x, back_y, arrived, *after)


def solve_modal(modal_buoy, modal_vel, wave, eig_val):
    diag_buoy = (1.0 + diffuse_buoy * wave) + diffuse_buoy * eig_val
    diag_vel = (1.0 + diffuse_vel * wave) + diffuse_vel * eig_val
    scale = 1.0 / (diag_buoy * diag_vel + couple_buoy * couple_vel)
    modal_buoy = modal_buoy * scale
    modal_vel = modal_vel * scale
    solved_buoy = (diag_vel * modal_buoy - couple_buoy * modal_vel).astype(BF16)
    solved_vel = (diag_buoy * modal_vel + couple_vel * modal_buoy).astype(BF16)
    return (solved_buoy, solved_vel)


def project(refs, field, proj_ref):
    blocks, _, _, span, lanes = refs[0].shape
    parts = [ref[:, field].reshape(blocks * ref.shape[2], span, lanes) for ref in refs]
    fluxes = jnp.concatenate(parts, axis=0).astype(F32)
    fluxes = jnp.swapaxes(fluxes, 0, 1).astype(BF16)
    rows = [jnp.transpose(fluxes[mode]) for mode in range(span)]
    return jnp.dot(jnp.concatenate(rows, axis=0), proj_ref[...], preferred_element_type=F32)


def finish_kernel(
    count,
    wave_x_ref,
    wave_y_ref,
    eig_val_ref,
    left_ref,
    right_ref,
    proj_ref,
    buoy_ref,
    vel_ref,
    *refs,
):
    in_refs, out_refs = refs[:count], refs[-2:]
    span, lanes, degree = buoy_ref.shape
    modal = []
    for field, coeff_ref in enumerate((buoy_ref, vel_ref)):
        tend = explicit_step * project(in_refs, field, proj_ref)
        rhs = coeff_ref[...].reshape(span * lanes, degree).astype(F32) + tend
        modal.append(jnp.dot(rhs.astype(BF16), left_ref[...], preferred_element_type=F32))
    first = pl.program_id(0) * span
    waves = [4.0 * (wave_x_ref[first + mode] + wave_y_ref[...]) for mode in range(span)]
    solved = solve_modal(modal[0], modal[1], jnp.concatenate(waves, axis=0), eig_val_ref[...])
    for values, out_ref in zip(solved, out_refs):
        result = jnp.dot(values, right_ref[...], preferred_element_type=F32).astype(BF16)
        out_ref[...] = result.reshape(span, lanes, degree)


def finish(
    kernels, start, size, parts, proj, buoy, vel_w, eigen, wave_x, wave_y, earlier
):
    eig_val, eig_left, eig_right = eigen
    modes_y, degree = buoy.shape[1:]
    wave_x = wave_x[start : start + size]
    if not kernels:
        taken = [part[:, :, :, start - first :][:, :, :, :size] for first, part in parts]
        taken = [
            jnp.transpose(part, (1, 0, 2, 3, 4)).reshape(2, -1, size, modes_y) for part in taken
        ]
        tend = jnp.einsum(
            "fzak,zn->fakn", jnp.concatenate(taken, axis=1), proj, preferred_element_type=F32
        )
        fields = jnp.stack([buoy, vel_w])[:, start : start + size].astype(F32)
        rhs = (fields + explicit_step * tend).astype(BF16)
        modal = jnp.einsum("fakn,nj->fakj", rhs, eig_left, preferred_element_type=F32)
        wave = 4.0 * (wave_x[:, None, None] + wave_y[None, :, None])
        results = [
            jnp.einsum("akj,jn->akn", values, eig_right, preferred_element_type=F32).astype(BF16)
            for values in solve_modal(modal[0], modal[1], wave, eig_val)
        ]
        if earlier:
            results = [jnp.concatenate(pair, axis=0) for pair in zip(earlier, results)]
        return results
    span = 8
    block = pl.BlockSpec((span, modes_y, degree), lambda a: (a + start // span, 0, 0))

    def part_spec(first, part):
        return pl.BlockSpec(
            (*part.shape[:3], span, modes_y), lambda a: (0, 0, 0, a + (start - first) // span, 0)
        )

    result = jax.ShapeDtypeStruct(buoy.shape, BF16)
    operands = [wave_x, wave_y[:, None], eig_val[None, :], eig_left, eig_right, proj, buoy, vel_w]
    operands += [part for _, part in parts]
    return pl.pallas_call(
        lambda *refs: finish_kernel(len(parts), *refs),
        grid=(size // span,),
        in_specs=[
            pl.BlockSpec(memory_space=pltpu.SMEM),
            whole((modes_y, 1)),
            whole((1, degree)),
            whole(eig_left.shape),
            whole(eig_right.shape),
            whole(proj.shape),
            block,
            block,
        ]
        + [part_spec(first, part) for first, part in parts]
        + [pl.BlockSpec(memory_space=pl.ANY)] * len(earlier),
        out_specs=[block, block],
        out_shape=[result, result],
        input_output_aliases={len(operands) + item: item for item in range(len(earlier))},
        compiler_params=params(1),
        cost_estimate=pl.CostEstimate(
            flops=4 * size * modes_y * degree * (proj.shape[0] + 2 * degree),
            bytes_accessed=size * modes_y * (8 * degree + 4 * proj.shape[0]),
            transcendentals=size * modes_y * degree,
        ),
        name="finish",
    )(*operands, *earlier)


def chunk_sizes(own):
    first = -(-own * 4 // 18)
    return [size for size in (first, own - first) if size]


def per_device(buoy, vel_w, strat, eig_val, eig_left, eig_right):
    row_count = lax.axis_size("row")
    col_count = lax.axis_size("col")
    blocks = row_count * col_count
    modes_x, modes_y, degree = buoy.shape
    total_x, total_y = modes_x * row_count, modes_y * col_count
    grid_x, grid_y = 3 * total_x // 2, 3 * total_y // 2
    shard = strat.shape[0]
    own = -(-shard // row_count)
    padding = own * row_count - shard
    kernels = modes_y % 128 == 0 and modes_x % 64 == 0 and degree % 128 == 0
    row = lax.axis_index("row")
    col = lax.axis_index("col")


    def by_device(table):
        table = table.reshape(col_count, shard, degree)
        table = np.pad(table, ((0, 0), (0, padding), (0, 0)))
        table = table.reshape(col_count, row_count // pair, pair, own, degree)
        return np.transpose(table, (2, 0, 1, 3, 4)).reshape(blocks, own, degree)


    pair = 2 if row_count % 2 == 0 else 1

    def slot_of(row, col):
        return (row % pair * col_count + col) * (row_count // pair) + row // pair

    slots = [[slot_of(row, col) for col in range(col_count)] for row in range(row_count)]
    group = np.argsort(np.array(slots).reshape(-1)).tolist()

    def exchange(values):
        return lax.all_to_all(
            values,
            ("row", "col"),
            split_axis=0,
            concat_axis=0,
            axis_index_groups=[group],
            tiled=True,
        )

    levels, slopes, projector = cheb_tables(degree, shard * col_count)
    forward_z = np.stack([by_device(levels.T), by_device(slopes.T)])
    backward_z = by_device(projector)
    along_x = jnp.asarray(np.ascontiguousarray(fourier_eval(total_x, grid_x).T))
    back_x = jnp.asarray(np.ascontiguousarray(fourier_proj(total_x, grid_x).T))
    along_y = jnp.asarray(fourier_eval(total_y, grid_y))
    back_y = jnp.asarray(np.ascontiguousarray(fourier_proj(total_y, grid_y)))
    strat_own = lax.dynamic_slice_in_dim(jnp.pad(strat, (0, padding)), row * own, own)

    sizes = chunk_sizes(own)
    stops = np.cumsum(sizes)
    pieces = [(int(stop - size), int(stop)) for size, stop in zip(sizes, stops)]
    arrived = []
    for start, stop in pieces:
        table = forward_z[:, :, start:stop].reshape(2, blocks * (stop - start), degree)
        arrived.append(exchange(lift(kernels, vel_w, buoy, jnp.asarray(table), blocks)))
    split = modes_x - modes_x // 8
    parts, after = [], []
    for values, (start, stop) in zip(arrived, pieces):
        splits = [split, modes_x - split] if stop == own else [modes_x]
        after = planes(
            kernels,
            values,
            strat_own[start:stop],
            along_y,
            along_x,
            back_x,
            back_y,
            slots,
            splits,
            after,
        )
        parts.append([exchange(fluxes) for fluxes in after])
    proj = [
        backward_z[:, start:stop].reshape(blocks * (stop - start), degree)
        for start, stop in pieces
    ]
    proj = jnp.asarray(np.concatenate(proj, axis=0))
    wave_x = wave_squares(total_x, row * modes_x, modes_x)
    wave_y = wave_squares(total_y, col * modes_y, modes_y)
    eigen = (eig_val, eig_left, eig_right)
    results = []
    for start, size, fluxes in ((0, split, parts[-1][0]), (split, modes_x - split, parts[-1][1])):
        held = [(0, part[0]) for part in parts[:-1]] + [(start, fluxes)]
        results = finish(
            kernels, start, size, held, proj, buoy, vel_w, eigen, wave_x, wave_y, results
        )
    return tuple(results)


def solution(mesh):
    in_specs = (P("row", "col", None), P("row", "col", None), P("col"), P(), P(), P())
    out_specs = (P("row", "col", None), P("row", "col", None))
    return jax.shard_map(
        per_device, mesh=mesh, in_specs=in_specs, out_specs=out_specs, check_vma=False
    )
```

```python
import math

import jax
import jax.numpy as jnp
import numpy as np
from jax import lax
from jax.experimental import pallas as pl
from jax.experimental.pallas import tpu as pltpu
from jax.sharding import PartitionSpec as P

explicit_step = 0.5
diffuse_buoy = 0.5
diffuse_vel = 0.25
couple_buoy = 0.7
couple_vel = 0.7

BF16 = jnp.bfloat16
F32 = jnp.float32
VMEM_BYTES = 63 * 1024 * 1024


def fourier_trig(modes, points):
    order = np.arange(modes, dtype=np.int32)
    freq = ((order + 1) // 2).astype(np.float32)
    place = np.arange(points, dtype=np.float32)
    angle = np.float32(2.0 * math.pi / points) * freq[:, None] * place[None, :]
    return (order, np.where((order % 2 == 0)[:, None], np.cos(angle), np.sin(angle)))


def fourier_eval(modes, points):
    order, values = fourier_trig(modes, points)
    return (values * np.float32(math.sqrt(2.0 / modes))).astype(BF16)


def fourier_proj(modes, points):
    order, values = fourier_trig(modes, points)
    weight = np.where(order == 0, 1.0 / points, 2.0 / points).astype(np.float32)
    return np.transpose(values * weight[:, None] * np.float32(math.sqrt(modes / 2.0))).astype(BF16)


def cheb_tables(degree, points):
    order = np.arange(degree, dtype=np.float32)
    theta = np.float32(math.pi) * (np.arange(points, dtype=np.float32) + np.float32(0.5)) / np.float32(points)
    angle = order[:, None] * theta[None, :]
    norm = np.float32(math.sqrt(2.0 / degree))
    levels = np.cos(angle) * norm
    slopes = -(order[:, None] / np.float32(degree)) * np.sin(angle) * norm
    weight = np.where(order == 0, 1.0 / points, 2.0 / points).astype(np.float32)
    projector = np.transpose(np.cos(angle) * weight[:, None] * np.float32(math.sqrt(degree / 2.0)))
    return (levels.astype(BF16), slopes.astype(BF16), projector.astype(BF16))


def wave_squares(modes, offset, count):
    order = offset + jnp.arange(count, dtype=jnp.int32)
    freq = ((order + 1) // 2).astype(F32) * (2.0 / modes)
    return freq * freq


def params(grid_rank):
    return pltpu.CompilerParams(
        dimension_semantics=("arbitrary",) * grid_rank, vmem_limit_bytes=VMEM_BYTES
    )


def whole(shape):
    return pl.BlockSpec(shape, lambda *_: (0,) * len(shape))


def lift_kernel(vel_ref, buoy_ref, table_ref, out_ref):
    blocks, fields, depth, span, lanes = out_ref.shape
    for field, source in enumerate((vel_ref, buoy_ref)):
        coeffs = source[...].reshape(span * lanes, source.shape[-1])
        values = lax.dot_general(
            table_ref[field], coeffs, (((1,), (1,)), ((), ())), preferred_element_type=F32
        )
        values = values.astype(BF16).reshape(blocks * depth, span, lanes)
        out_ref[:, field] = values.reshape(blocks, depth, span, lanes)


def lift(kernels, vel_w, buoy, table, blocks):
    modes_x, modes_y, degree = vel_w.shape
    depth = table.shape[1] // blocks
    shape = (blocks, 2, depth, modes_x, modes_y)
    if not kernels:
        fields = jnp.stack([vel_w, buoy])
        values = jnp.einsum("fzn,fakn->fzak", table, fields, preferred_element_type=F32)
        values = values.astype(BF16).reshape(2, blocks, depth, modes_x, modes_y)
        return jnp.transpose(values, (1, 0, 2, 3, 4))
    span = 16
    return pl.pallas_call(
        lift_kernel,
        grid=(modes_x // span,),
        in_specs=[
            pl.BlockSpec((span, modes_y, degree), lambda a: (a, 0, 0)),
            pl.BlockSpec((span, modes_y, degree), lambda a: (a, 0, 0)),
            whole(table.shape),
        ],
        out_specs=pl.BlockSpec((blocks, 2, depth, span, modes_y), lambda a: (0, 0, 0, a, 0)),
        out_shape=jax.ShapeDtypeStruct(shape, BF16),
        compiler_params=params(1),
        cost_estimate=pl.CostEstimate(
            flops=2 * math.prod(shape) * degree,
            bytes_accessed=2 * (2 * vel_w.size + math.prod(shape)),
            transcendentals=0,
        ),
        name="lift",
    )(vel_w, buoy, table)


def plane_kernel(
    col_count, count, strat_ref, along_y_ref, along_x_ref, back_x_ref, back_y_ref, in_ref, *refs
):
    out_refs = refs[-count:]
    blocks, _, depth, modes_x, lanes = in_ref.shape
    row_count = blocks // col_count
    for level in range(depth):
        grids = []
        for field in range(2):
            rows = []
            for row in range(row_count):
                parts = [in_ref[col * row_count + row, field, level] for col in range(col_count)]
                rows.append(jnp.concatenate(parts, axis=1))
            middle = jnp.dot(
                jnp.concatenate(rows, axis=0), along_y_ref[...], preferred_element_type=F32
            ).astype(BF16)
            grid = jnp.dot(along_x_ref[...], middle, preferred_element_type=F32)
            grids.append(grid.astype(BF16).astype(F32))
        velocity, gradient = grids
        strata = strat_ref[pl.program_id(0) * depth + level]
        flux_buoy = (-(velocity * gradient) - strata * velocity).astype(BF16)
        flux_vel = (-(velocity * jnp.abs(velocity))).astype(BF16)
        for field, flux in enumerate((flux_buoy, flux_vel)):
            folded = jnp.dot(back_x_ref[...], flux, preferred_element_type=F32).astype(BF16)
            values = jnp.dot(folded, back_y_ref[...], preferred_element_type=F32).astype(BF16)
            for row in range(row_count):
                first = row * modes_x
                for out_ref in out_refs:
                    last = first + out_ref.shape[3]
                    for col in range(col_count):
                        out_ref[col * row_count + row, field, level] = values[
                            first:last, col * lanes : (col + 1) * lanes
                        ]
                    first = last


def planes(kernels, arrived, strat, along_y, along_x, back_x, back_y, col_count, splits, after):
    blocks, fields, depth, modes_x, modes_y = arrived.shape
    row_count = blocks // col_count
    if not kernels:
        parts = arrived.reshape(col_count, row_count, fields, depth, modes_x, modes_y)
        parts = jnp.transpose(parts, (2, 3, 1, 4, 0, 5))
        parts = parts.reshape(fields, depth, row_count * modes_x, col_count * modes_y)
        middle = jnp.einsum("fzak,ky->fzay", parts, along_y, preferred_element_type=F32)
        grids = jnp.einsum("xa,fzay->fzxy", along_x, middle.astype(BF16), preferred_element_type=F32)
        grids = grids.astype(BF16).astype(F32)
        flux_buoy = -(grids[0] * grids[1]) - strat[:, None, None] * grids[0]
        flux_vel = -(grids[0] * jnp.abs(grids[0]))
        fluxes = jnp.stack([flux_buoy, flux_vel]).astype(BF16)
        folded = jnp.einsum("ax,fzxy->fzay", back_x, fluxes, preferred_element_type=F32)
        values = jnp.einsum("fzay,yk->fzak", folded.astype(BF16), back_y, preferred_element_type=F32)
        values = values.astype(BF16).reshape(
            fields, depth, row_count, modes_x, col_count, modes_y
        )
        values = jnp.transpose(values, (4, 2, 0, 1, 3, 5)).reshape(arrived.shape)
        return jnp.split(values, np.cumsum(splits)[:-1], axis=3)
    block = pl.BlockSpec((blocks, fields, 1, modes_x, modes_y), lambda z: (0, 0, z, 0, 0))
    work = along_y.size * along_x.shape[1] + along_x.size * along_y.shape[1]
    return pl.pallas_call(
        lambda *refs: plane_kernel(col_count, len(splits), *refs),
        grid=(depth,),
        in_specs=[
            pl.BlockSpec(memory_space=pltpu.SMEM),
            whole(along_y.shape),
            whole(along_x.shape),
            whole(back_x.shape),
            whole(back_y.shape),
            block,
        ]
        + [pl.BlockSpec(memory_space=pl.ANY)] * len(after),
        out_specs=[
            pl.BlockSpec((blocks, fields, 1, size, modes_y), lambda z: (0, 0, z, 0, 0))
            for size in splits
        ],
        out_shape=[
            jax.ShapeDtypeStruct((blocks, fields, depth, size, modes_y), BF16) for size in splits
        ],
        compiler_params=params(1),
        cost_estimate=pl.CostEstimate(
            flops=4 * fields * depth * work, bytes_accessed=4 * arrived.size, transcendentals=0
        ),
        name="planes",
    )(strat, along_y, along_x, back_x, back_y, arrived, *after)


def solve_modal(modal_buoy, modal_vel, wave, eig_val):
    diag_buoy = (1.0 + diffuse_buoy * wave) + diffuse_buoy * eig_val
    diag_vel = (1.0 + diffuse_vel * wave) + diffuse_vel * eig_val
    scale = 1.0 / (diag_buoy * diag_vel + couple_buoy * couple_vel)
    modal_buoy = modal_buoy * scale
    modal_vel = modal_vel * scale
    solved_buoy = (diag_vel * modal_buoy - couple_buoy * modal_vel).astype(BF16)
    solved_vel = (diag_buoy * modal_vel + couple_vel * modal_buoy).astype(BF16)
    return (solved_buoy, solved_vel)


def project(refs, field, proj_ref):
    blocks, _, _, span, lanes = refs[0].shape
    parts = [ref[:, field].reshape(blocks * ref.shape[2], span, lanes) for ref in refs]
    fluxes = jnp.swapaxes(jnp.concatenate(parts, axis=0), 0, 1)
    rows = [jnp.transpose(fluxes[mode]) for mode in range(span)]
    return jnp.dot(jnp.concatenate(rows, axis=0), proj_ref[...], preferred_element_type=F32)


def finish_kernel(
    count,
    wave_x_ref,
    wave_y_ref,
    eig_val_ref,
    left_ref,
    right_ref,
    proj_ref,
    buoy_ref,
    vel_ref,
    *refs,
):
    in_refs, out_refs = refs[:count], refs[-2:]
    span, lanes, degree = buoy_ref.shape
    modal = []
    for field, coeff_ref in enumerate((buoy_ref, vel_ref)):
        tend = explicit_step * project(in_refs, field, proj_ref)
        rhs = coeff_ref[...].reshape(span * lanes, degree).astype(F32) + tend
        modal.append(jnp.dot(rhs.astype(BF16), left_ref[...], preferred_element_type=F32))
    first = pl.program_id(0) * span
    waves = [4.0 * (wave_x_ref[first + mode] + wave_y_ref[...]) for mode in range(span)]
    solved = solve_modal(modal[0], modal[1], jnp.concatenate(waves, axis=0), eig_val_ref[...])
    for values, out_ref in zip(solved, out_refs):
        result = jnp.dot(values, right_ref[...], preferred_element_type=F32).astype(BF16)
        out_ref[...] = result.reshape(span, lanes, degree)


def finish(
    kernels, start, size, parts, proj, buoy, vel_w, eigen, wave_x, wave_y, earlier
):
    eig_val, eig_left, eig_right = eigen
    modes_y, degree = buoy.shape[1:]
    wave_x = wave_x[start : start + size]
    if not kernels:
        taken = [part[:, :, :, start - first :][:, :, :, :size] for first, part in parts]
        taken = [
            jnp.transpose(part, (1, 0, 2, 3, 4)).reshape(2, -1, size, modes_y) for part in taken
        ]
        tend = jnp.einsum(
            "fzak,zn->fakn", jnp.concatenate(taken, axis=1), proj, preferred_element_type=F32
        )
        fields = jnp.stack([buoy, vel_w])[:, start : start + size].astype(F32)
        rhs = (fields + explicit_step * tend).astype(BF16)
        modal = jnp.einsum("fakn,nj->fakj", rhs, eig_left, preferred_element_type=F32)
        wave = 4.0 * (wave_x[:, None, None] + wave_y[None, :, None])
        results = [
            jnp.einsum("akj,jn->akn", values, eig_right, preferred_element_type=F32).astype(BF16)
            for values in solve_modal(modal[0], modal[1], wave, eig_val)
        ]
        if earlier:
            results = [jnp.concatenate(pair, axis=0) for pair in zip(earlier, results)]
        return results
    span = 8
    block = pl.BlockSpec((span, modes_y, degree), lambda a: (a + start // span, 0, 0))

    def part_spec(first, part):
        return pl.BlockSpec(
            (*part.shape[:3], span, modes_y), lambda a: (0, 0, 0, a + (start - first) // span, 0)
        )

    result = jax.ShapeDtypeStruct(buoy.shape, BF16)
    operands = [wave_x, wave_y[:, None], eig_val[None, :], eig_left, eig_right, proj, buoy, vel_w]
    operands += [part for _, part in parts]
    return pl.pallas_call(
        lambda *refs: finish_kernel(len(parts), *refs),
        grid=(size // span,),
        in_specs=[
            pl.BlockSpec(memory_space=pltpu.SMEM),
            whole((modes_y, 1)),
            whole((1, degree)),
            whole(eig_left.shape),
            whole(eig_right.shape),
            whole(proj.shape),
            block,
            block,
        ]
        + [part_spec(first, part) for first, part in parts]
        + [pl.BlockSpec(memory_space=pl.ANY)] * len(earlier),
        out_specs=[block, block],
        out_shape=[result, result],
        input_output_aliases={len(operands) + item: item for item in range(len(earlier))},
        compiler_params=params(1),
        cost_estimate=pl.CostEstimate(
            flops=4 * size * modes_y * degree * (proj.shape[0] + 2 * degree),
            bytes_accessed=size * modes_y * (8 * degree + 4 * proj.shape[0]),
            transcendentals=size * modes_y * degree,
        ),
        name="finish",
    )(*operands, *earlier)


def chunk_sizes(own):
    first = -(-own * 4 // 18)
    return [size for size in (first, own - first) if size]


def per_device(buoy, vel_w, strat, eig_val, eig_left, eig_right):
    row_count = lax.axis_size("row")
    col_count = lax.axis_size("col")
    blocks = row_count * col_count
    modes_x, modes_y, degree = buoy.shape
    total_x, total_y = modes_x * row_count, modes_y * col_count
    grid_x, grid_y = 3 * total_x // 2, 3 * total_y // 2
    shard = strat.shape[0]
    own = -(-shard // row_count)
    padding = own * row_count - shard
    kernels = modes_y % 128 == 0 and modes_x % 64 == 0 and degree % 128 == 0
    row = lax.axis_index("row")
    col = lax.axis_index("col")


    def by_device(table):
        table = table.reshape(col_count, shard, degree)
        table = np.pad(table, ((0, 0), (0, padding), (0, 0)))
        return table.reshape(blocks, own, degree)

    def exchange(values):
        return lax.all_to_all(values, ("col", "row"), split_axis=0, concat_axis=0, tiled=True)

    levels, slopes, projector = cheb_tables(degree, shard * col_count)
    forward_z = np.stack([by_device(levels.T), by_device(slopes.T)])
    backward_z = by_device(projector)
    along_x = jnp.asarray(np.ascontiguousarray(fourier_eval(total_x, grid_x).T))
    back_x = jnp.asarray(np.ascontiguousarray(fourier_proj(total_x, grid_x).T))
    along_y = jnp.asarray(fourier_eval(total_y, grid_y))
    back_y = jnp.asarray(np.ascontiguousarray(fourier_proj(total_y, grid_y)))
    strat_own = lax.dynamic_slice_in_dim(jnp.pad(strat, (0, padding)), row * own, own)

    sizes = chunk_sizes(own)
    stops = np.cumsum(sizes)
    pieces = [(int(stop - size), int(stop)) for size, stop in zip(sizes, stops)]
    arrived = []
    for start, stop in pieces:
        table = forward_z[:, :, start:stop].reshape(2, blocks * (stop - start), degree)
        arrived.append(exchange(lift(kernels, vel_w, buoy, jnp.asarray(table), blocks)))
    split = modes_x - modes_x // 8
    parts, after = [], []
    for values, (start, stop) in zip(arrived, pieces):
        splits = [split, modes_x - split] if stop == own else [modes_x]
        after = planes(
            kernels,
            values,
            strat_own[start:stop],
            along_y,
            along_x,
            back_x,
            back_y,
            col_count,
            splits,
            after,
        )
        parts.append([exchange(fluxes) for fluxes in after])
    proj = [
        backward_z[:, start:stop].reshape(blocks * (stop - start), degree)
        for start, stop in pieces
    ]
    proj = jnp.asarray(np.concatenate(proj, axis=0))
    wave_x = wave_squares(total_x, row * modes_x, modes_x)
    wave_y = wave_squares(total_y, col * modes_y, modes_y)
    eigen = (eig_val, eig_left, eig_right)
    results = []
    for start, size, fluxes in ((0, split, parts[-1][0]), (split, modes_x - split, parts[-1][1])):
        held = [(0, part[0]) for part in parts[:-1]] + [(start, fluxes)]
        results = finish(
            kernels, start, size, held, proj, buoy, vel_w, eigen, wave_x, wave_y, results
        )
    return tuple(results)


def solution(mesh):
    in_specs = (P("row", "col", None), P("row", "col", None), P("col"), P(), P(), P())
    out_specs = (P("row", "col", None), P("row", "col", None))
    return jax.shard_map(
        per_device, mesh=mesh, in_specs=in_specs, out_specs=out_specs, check_vma=False
    )
```
